32 devices in a mesh: shape: 2 (over x), query: 16 (over z, y, core).
Axes of the slice: x: 2, y: 2, z: 4, core: 2. Of those that a mesh axis runs over, the one named last changes fastest.
Arguments:
- latents: bfloat16 [512, 1024], P(('shape', 'query')), parts along dimension 0, may hold values from -6 to 6
- gain_self: float32 [1024], replicated, may hold values from 1.5 to 4, as said below
- w_qkv: bfloat16 [3, 1024, 1024], P(None, 'query'), may hold values from -0.1875 to 0.1875
- w_out: bfloat16 [1024, 1024], P('query'), may hold values from -0.1875 to 0.1875
- gain_cross: float32 [1024], replicated, may hold values from 1.5 to 4, as said below
- w_kv: bfloat16 [2, 1024, 1024], replicated, may hold values from -0.1875 to 0.1875
- w_embed: bfloat16 [51, 1024], replicated, may hold values from -0.875 to 0.875
- gain_point: float32 [1024], replicated, may hold values from 1.5 to 4, as said below
- w_query: bfloat16 [1024, 1024], replicated, may hold values from -0.1875 to 0.1875
- w_back: bfloat16 [1024, 1024], replicated, may hold values from -0.1875 to 0.1875
- gain_head: float32 [1024], replicated, may hold values from 0.5 to 1.5
- w_hidden: bfloat16 [1024, 1024], replicated, may hold values from -0.1875 to 0.1875
- w_sdf: bfloat16 [1024], replicated, may hold values from -0.1875 to 0.1875
Outputs:
- decoded: bfloat16 [512, 1024], P(('shape', 'query')), parts along dimension 0
- sdf: float32 [32768], P(('shape', 'query')), parts along dimension 0
The draws below stay inside these ranges and needn't reach their ends.
There are 2 independent parts, one for each index of `shape`. The reference program is written for one: setup_inputs(seed, part) draws one part's arguments, and reference() takes and returns one part's arrays. A program takes and returns all parts, laid end to end along the dimension named above; an argument that names none is the same for every part. Nothing has to cross between parts.
Inputs may be any that keep to these rules, and one draw needn't show every extreme that they name: `gain_self`: per-channel norm gains. `gain_cross`: per-channel norm gains. `gain_point`: per-channel norm gains.
All inputs are finite; a program needn't handle non-finite values.
Results may differ from the reference program's by a relative error of at most 0.023.
The reference program's roundings to bfloat16 on the way count: a program that leaves them out, or rounds other values in their place, can miss the bound.
Values may be sent and summed in bfloat16 or wider, within the bound.
No kernel may reach another device: no remote copies, remote signals or barrier semaphores. Data moves between devices by JAX's collectives and lax.ppermute only.
A program may use at most 128 MiB of HBM per device.

```python
import math
import jax
import jax.numpy as jnp
from jax import lax

D = 1024
HEADS = 16
FREQS = 8
GRID = 512
PTS_DEV = 1024
FE = 51
NLAT = 256
NPTS = 16384
N_QUERY = 16


def gain_law(key):
    return jax.random.uniform(key, (D,), jnp.float32, 1.5, 2.6)


def draw_gain_self(key, part):
    return gain_law(jax.random.fold_in(key, 11))


def draw_gain_cross(key, part):
    return gain_law(jax.random.fold_in(key, 23))


def draw_gain_point(key, part):
    return gain_law(jax.random.fold_in(key, 37))


def level_of(stream_key, dims, shards, smallest, top_value):
    def one(position, parts):
        draws = jax.random.uniform(jax.random.fold_in(jax.random.fold_in(stream_key, 6), position), (parts,), jnp.float32, smallest / len(shards), top_value / len(shards))
        return jnp.repeat(jnp.exp(draws), dims[position] // parts).reshape((-1,) + (1,) * (len(dims) - position - 1))

    level = one(*shards[0])
    for cut in shards[1:]:
        level = level * one(*cut)
    return level


def bell_draw(stream_key, shape, deviation, most, shards=(), kind=jnp.bfloat16):
    drawn = jax.random.normal(stream_key, shape, jnp.float32) * deviation
    if len(shards) > 0:
        drawn = level_of(stream_key, shape, shards, -0.22, 0.18) * drawn
    return jnp.clip(drawn, min=-most, max=most).astype(kind)


def setup_inputs(seed: int = 0, part: int = 0) -> dict:
    key_list = jax.random.split(jax.random.key(seed), 14)
    own_keys = jax.random.split(jax.random.fold_in(key_list[13], part), 14)
    latents = bell_draw(own_keys[0], (NLAT, D), 1.0, 6.0, ((0, 16),))
    gain_self = draw_gain_self(jax.random.fold_in(key_list[13], 71), part)
    w_qkv = bell_draw(key_list[2], (3, D, D), D ** -0.5, 0.1875, ((1, 16),))
    w_out = bell_draw(key_list[3], (D, D), D ** -0.5, 0.1875, ((0, 16),))
    gain_cross = draw_gain_cross(jax.random.fold_in(key_list[13], 71), part)
    w_kv = bell_draw(key_list[5], (2, D, D), D ** -0.5, 0.1875)
    w_embed = bell_draw(key_list[6], (FE, D), FE ** -0.5, 0.875)
    gain_point = draw_gain_point(jax.random.fold_in(key_list[13], 71), part)
    w_query = bell_draw(key_list[8], (D, D), D ** -0.5, 0.1875)
    w_back = bell_draw(key_list[9], (D, D), D ** -0.5, 0.1875)
    gain_head = jnp.clip(1.0 + 0.1 * jax.random.normal(key_list[10], (D,), jnp.float32), 0.5, 1.5)
    w_hidden = bell_draw(key_list[11], (D, D), D ** -0.5, 0.1875)
    w_sdf = bell_draw(key_list[12], (D,), D ** -0.5, 0.1875)
    return {"latents": latents, "gain_self": gain_self, "w_qkv": w_qkv, "w_out": w_out, "gain_cross": gain_cross, "w_kv": w_kv, "w_embed": w_embed, "gain_point": gain_point, "w_query": w_query, "w_back": w_back, "gain_head": gain_head, "w_hidden": w_hidden, "w_sdf": w_sdf}


def norm_rows(values, gain):
    center = lax.optimization_barrier(jnp.mean(values, axis=-1, keepdims=True))
    centred = values - center
    spread = lax.optimization_barrier(jnp.mean(centred * centred, axis=-1, keepdims=True))
    return centred * lax.rsqrt(spread + 1e-05) * gain

def attend(queries, keys, values):
    row_count, features = queries.shape
    key_count = keys.shape[0]
    head_dim = features // HEADS
    group_count = HEADS // 4
    head_queries = queries.reshape(row_count, group_count, 4, head_dim).transpose(1, 0, 2, 3)
    head_keys = keys.reshape(key_count, group_count, 4, head_dim).transpose(1, 0, 2, 3)
    head_values = values.reshape(key_count, group_count, 4, head_dim).transpose(1, 0, 2, 3)
    scaling = 1.0 / math.sqrt(head_dim)

    def per_group(block):
        group_query, group_keys, group_values = block
        scores = jnp.einsum('rge,nge->grn', group_query.astype(jnp.float32), group_keys.astype(jnp.float32)) * scaling
        highest = lax.optimization_barrier(jnp.max(scores, axis=-1, keepdims=True))
        powers = jnp.exp(scores - highest)
        total = lax.optimization_barrier(jnp.sum(powers, axis=-1, keepdims=True))
        weights = (powers / total).astype(jnp.bfloat16)
        blended = jnp.einsum('grn,nge->rge', weights.astype(jnp.float32), group_values.astype(jnp.float32))
        return blended.astype(jnp.bfloat16)
    result = lax.map(per_group, (head_queries, head_keys, head_values))
    return result.transpose(1, 0, 2, 3).reshape(row_count, features)

def point_features(numbers):
    cell_i = numbers // (GRID * GRID)
    cell_j = numbers // GRID % GRID
    cell_k = numbers % GRID
    cells = jnp.stack([cell_i, cell_j, cell_k], axis=1).astype(jnp.float32)
    coords = (2.0 * cells + 1.0) / GRID - 1.0
    freqs = 2.0 ** jnp.arange(FREQS, dtype=jnp.float32) * math.pi
    angles = (coords[:, :, None] * freqs[None, None, :]).reshape(numbers.shape[0], 3 * FREQS)
    return jnp.concatenate([coords, jnp.sin(angles), jnp.cos(angles)], axis=1).astype(jnp.bfloat16)

def decode_points(numbers, keys, values, w_embed, gain_point, w_query, w_back, gain_head, w_hidden, w_sdf):
    features = point_features(numbers)
    embedded = jnp.dot(features, w_embed, preferred_element_type=jnp.float32)
    normed = norm_rows(embedded, gain_point).astype(jnp.bfloat16)
    point_query = jnp.dot(normed, w_query, preferred_element_type=jnp.float32).astype(jnp.bfloat16)
    crossed = attend(point_query, keys, values)
    joined = embedded + jnp.dot(crossed, w_back, preferred_element_type=jnp.float32)
    head_in = norm_rows(joined, gain_head).astype(jnp.bfloat16)
    hidden = jax.nn.gelu(jnp.dot(head_in, w_hidden, preferred_element_type=jnp.float32)).astype(jnp.bfloat16)
    return jnp.dot(hidden, w_sdf, preferred_element_type=jnp.float32)

def reference(latents, gain_self, w_qkv, w_out, gain_cross, w_kv, w_embed, gain_point, w_query, w_back, gain_head, w_hidden, w_sdf):
    inputs = latents.astype(jnp.float32)
    normed = norm_rows(inputs, gain_self).astype(jnp.bfloat16)
    qkv = jnp.einsum('rd,sdc->src', normed.astype(jnp.float32), w_qkv.astype(jnp.float32)).astype(jnp.bfloat16)
    attended = attend(qkv[0], qkv[1], qkv[2])
    decoded = (inputs + jnp.dot(attended, w_out, preferred_element_type=jnp.float32)).astype(jnp.bfloat16)
    normed_two = norm_rows(decoded.astype(jnp.float32), gain_cross).astype(jnp.bfloat16)
    keys_values = jnp.einsum('rd,sdc->src', normed_two.astype(jnp.float32), w_kv.astype(jnp.float32)).astype(jnp.bfloat16)

    def decode_block(block_index):
        numbers = block_index * PTS_DEV + jnp.arange(PTS_DEV, dtype=jnp.int32)
        return decode_points(numbers, keys_values[0], keys_values[1], w_embed, gain_point, w_query, w_back, gain_head, w_hidden, w_sdf)
    sdf = lax.map(decode_block, jnp.arange(N_QUERY, dtype=jnp.int32)).reshape(NPTS)
    return (decoded, sdf)
```

```python
import functools
import math

import jax
import jax.numpy as jnp
from jax import lax
from jax.experimental import pallas as pl
from jax.experimental.pallas import tpu as pltpu
from jax.sharding import PartitionSpec as P

HEADS = 16
FREQS = 8
GRID = 512
HEAD_DIM = 64
SCALE = 1.0 / math.sqrt(HEAD_DIM)
POINT_BLOCK = 256
VMEM_LIMIT = 40 * 1024 * 1024
FEATURE_ROWS = 64


def norm_rows(values, gain):
    center = jnp.mean(values, axis=-1, keepdims=True)
    centred = values - center
    spread = jnp.mean(centred * centred, axis=-1, keepdims=True)
    return centred * lax.rsqrt(spread + 1e-05) * gain


def attend(queries, keys, values):
    row_count, features = queries.shape
    key_count = keys.shape[0]
    head_dim = features // HEADS
    group_count = HEADS // 4
    head_queries = queries.reshape(row_count, group_count, 4, head_dim).transpose(1, 0, 2, 3)
    head_keys = keys.reshape(key_count, group_count, 4, head_dim).transpose(1, 0, 2, 3)
    head_values = values.reshape(key_count, group_count, 4, head_dim).transpose(1, 0, 2, 3)
    scaling = 1.0 / math.sqrt(head_dim)

    def per_group(block):
        group_query, group_keys, group_values = block
        scores = (
            jnp.einsum("rge,nge->grn", group_query, group_keys, preferred_element_type=jnp.float32)
            * scaling
        )
        highest = jnp.max(scores, axis=-1, keepdims=True)
        powers = jnp.exp(scores - highest)
        total = jnp.sum(powers, axis=-1, keepdims=True)
        weights = (powers / total).astype(jnp.bfloat16)
        blended = jnp.einsum(
            "grn,nge->rge", weights, group_values, preferred_element_type=jnp.float32
        )
        return blended.astype(jnp.bfloat16)

    result = lax.map(per_group, (head_queries, head_keys, head_values))
    return result.transpose(1, 0, 2, 3).reshape(row_count, features)


def feature_rows(numbers):
    cell_i = numbers // (GRID * GRID)
    cell_j = numbers // GRID % GRID
    cell_k = numbers % GRID
    cells = jnp.stack([cell_i, cell_j, cell_k], axis=0).astype(jnp.float32)
    coords = (2.0 * cells + 1.0) / GRID - 1.0
    freqs = 2.0 ** jnp.arange(FREQS, dtype=jnp.float32) * math.pi
    angles = (coords[:, None, :] * freqs[None, :, None]).reshape(3 * FREQS, numbers.shape[0])
    return jnp.concatenate([coords, jnp.sin(angles), jnp.cos(angles)], axis=0).astype(jnp.bfloat16)


def any_slice(
    latents, gain_self, w_qkv, w_out, gain_cross, w_kv, w_embed, gain_point, w_query, w_back,
    gain_head, w_hidden, w_sdf, *, points,
):
    inputs = latents.astype(jnp.float32)
    normed = norm_rows(inputs, gain_self).astype(jnp.bfloat16)
    qkv = jnp.einsum(
        "rd,sdc->src",
        normed,
        lax.all_gather(w_qkv, "query", axis=1, tiled=True),
        preferred_element_type=jnp.float32,
    ).astype(jnp.bfloat16)
    self_keys, self_values = (
        lax.all_gather(qkv[1], "query", axis=0, tiled=True),
        lax.all_gather(qkv[2], "query", axis=0, tiled=True),
    )
    attended = attend(qkv[0], self_keys, self_values)
    update = jnp.dot(
        attended,
        lax.all_gather(w_out, "query", axis=0, tiled=True),
        preferred_element_type=jnp.float32,
    )
    decoded = (inputs + update).astype(jnp.bfloat16)
    normed_two = norm_rows(decoded.astype(jnp.float32), gain_cross).astype(jnp.bfloat16)
    stacked = jnp.einsum(
        "rd,sdc->src",
        lax.all_gather(normed_two, "query", axis=0, tiled=True),
        w_kv,
        preferred_element_type=jnp.float32,
    ).astype(jnp.bfloat16)
    numbers = lax.axis_index("query") * points + jnp.arange(points, dtype=jnp.int32)
    features = feature_rows(numbers).T
    embedded = jnp.dot(features, w_embed, preferred_element_type=jnp.float32)
    point_normed = norm_rows(embedded, gain_point).astype(jnp.bfloat16)
    point_query = jnp.dot(point_normed, w_query, preferred_element_type=jnp.float32).astype(
        jnp.bfloat16
    )
    crossed = attend(point_query, stacked[0], stacked[1])
    joined = embedded + jnp.dot(crossed, w_back, preferred_element_type=jnp.float32)
    head_in = norm_rows(joined, gain_head).astype(jnp.bfloat16)
    hidden = jax.nn.gelu(jnp.dot(head_in, w_hidden, preferred_element_type=jnp.float32)).astype(
        jnp.bfloat16
    )
    sdf = jnp.dot(hidden, w_sdf, preferred_element_type=jnp.float32)
    return (decoded, sdf)


def dot_nn(left, right):
    return lax.dot_general(left, right, (((1,), (0,)), ((), ())), preferred_element_type=jnp.float32)


def dot_nt(left, right):
    return lax.dot_general(left, right, (((1,), (1,)), ((), ())), preferred_element_type=jnp.float32)


def dot_tn(left, right):
    return lax.dot_general(left, right, (((0,), (0,)), ((), ())), preferred_element_type=jnp.float32)


def pack_kernel(w_ref, latents_ref, out_ref):
    rows = w_ref.shape[1]
    for target in range(HEADS):
        low = target * HEAD_DIM
        first = 512 * (target % 2)
        beside = [
            latents_ref[:, first + 256 + 64 * part : first + 320 + 64 * part] for part in range(4)
        ]
        pieces = [w_ref[s, :, low : low + HEAD_DIM] for s in range(3)]
        pieces.append(jnp.concatenate(beside, axis=0))
        out_ref[target, :rows, :] = jnp.concatenate(pieces, axis=1)
        out_ref[target, rows:, :] = latents_ref[:, first : first + 256]


def pack(w_qkv, latents):
    rows = w_qkv.shape[1]
    return pl.pallas_call(
        pack_kernel,
        out_shape=jax.ShapeDtypeStruct((HEADS, rows + 16, 256), jnp.bfloat16),
        name="pack",
    )(w_qkv, latents)


def unpack_kernel(received_ref, half_ref):
    rows = half_ref.shape[0]
    parts = [received_ref[:, 64:80, :].reshape(rows, 256)]
    for part in range(4):
        parts.append(received_ref[:, 16 * part : 16 * part + 16, 192:256].reshape(rows, 64))
    half_ref[...] = jnp.concatenate(parts, axis=1)


def unpack(received):
    rows = received.shape[0] * 16
    return pl.pallas_call(
        unpack_kernel,
        out_shape=jax.ShapeDtypeStruct((rows, 512), jnp.bfloat16),
        name="unpack",
    )(received)


def point_kernel(features_ref, w_embed_ref, gain_ref, w_query_ref, out_ref):
    embedded = dot_tn(features_ref[...], w_embed_ref[...])
    normed = norm_rows(embedded, gain_ref[...]).astype(jnp.bfloat16)
    out_ref[...] = dot_nn(normed, w_query_ref[...]).astype(jnp.bfloat16)


def point_queries(features, w_embed, gain, w_query):
    points = features.shape[1]
    width = w_query.shape[1]
    return pl.pallas_call(
        point_kernel,
        grid=(points // POINT_BLOCK,),
        in_specs=[
            pl.BlockSpec((FEATURE_ROWS, POINT_BLOCK), lambda i: (0, i)),
            pl.BlockSpec((FEATURE_ROWS, width), lambda i: (0, 0)),
            pl.BlockSpec((1, width), lambda i: (0, 0)),
            pl.BlockSpec((width, width), lambda i: (0, 0)),
        ],
        out_specs=pl.BlockSpec((POINT_BLOCK, width), lambda i: (i, 0)),
        out_shape=jax.ShapeDtypeStruct((points, width), jnp.bfloat16),
        cost_estimate=pl.CostEstimate(
            flops=2 * points * width * (width + FEATURE_ROWS),
            bytes_accessed=4 * width * width,
            transcendentals=0,
        ),
        name="point_queries",
    )(features, w_embed, gain, w_query)


def self_kernel(core_ref, received_ref, own_ref, other_ref, gain_ref, attended_ref, latents_ref):
    sources = received_ref.shape[0]
    first = core_ref[0] == 0
    own, other = own_ref[...], other_ref[...]
    latents = jnp.concatenate(
        [jnp.where(first, own, other), jnp.where(first, other, own)], axis=1
    )
    latents_ref[...] = latents
    normed = norm_rows(latents.astype(jnp.float32), gain_ref[...]).astype(jnp.bfloat16)
    weights = received_ref[:, :64, :].reshape(sources * 64, 256)
    qkv = dot_nn(normed, weights).astype(jnp.bfloat16)
    queries, keys = qkv[:, :64], qkv[:, 64:128]
    values = qkv[:, 128:192]
    scores = dot_nt(keys, queries) * SCALE
    powers = jnp.exp(scores - jnp.max(scores, axis=0, keepdims=True))
    shares = (powers / jnp.sum(powers, axis=0, keepdims=True)).astype(jnp.bfloat16)
    attended_ref[...] = dot_tn(values, shares).astype(jnp.bfloat16)


def self_attention(core, received, own, other, gain):
    rows = received.shape[0] * 16
    vmem = pl.BlockSpec(memory_space=pltpu.VMEM)
    return pl.pallas_call(
        self_kernel,
        in_specs=[pl.BlockSpec(memory_space=pltpu.SMEM)] + [vmem] * 4,
        out_shape=(
            jax.ShapeDtypeStruct((HEAD_DIM, rows), jnp.bfloat16),
            jax.ShapeDtypeStruct((rows, gain.shape[1]), jnp.bfloat16),
        ),
        name="self_attention",
    )(core, received, own, other, gain)


def tail_kernel(
    first_ref, near_ref, far_ref, out_near_ref, out_far_ref, latents_ref, gain_cross_ref, w_kv_ref,
    queries_ref, features_ref, w_back_ref, w_embed_ref, gain_head_ref, w_hidden_ref, w_sdf_ref,
    decoded_ref, sdf_ref, all_decoded, key_pairs, value_rows, crossed,
):
    width = latents_ref.shape[1]
    update = dot_tn(near_ref[...], out_near_ref[...]) + dot_tn(far_ref[...], out_far_ref[...])
    decoded = (latents_ref[...].astype(jnp.float32) + update).astype(jnp.bfloat16)
    all_decoded[...] = decoded
    decoded_ref[...] = all_decoded[pl.ds(pl.multiple_of(first_ref[0], 16), 16), :]
    normed = norm_rows(decoded.astype(jnp.float32), gain_cross_ref[...]).astype(jnp.bfloat16)
    keys = dot_nn(normed, w_kv_ref[0]).astype(jnp.bfloat16) * SCALE
    key_count = keys.shape[0]
    lane = lax.broadcasted_iota(jnp.int32, (key_count, 128), 1)
    for pair in range(HEADS // 2):
        both = keys[:, 128 * pair : 128 * pair + 128]
        zero = jnp.zeros_like(both)
        key_pairs[pair, :key_count, :] = jnp.where(lane < HEAD_DIM, both, zero)
        key_pairs[pair, key_count:, :] = jnp.where(lane < HEAD_DIM, zero, both)
    values = dot_nn(normed, w_kv_ref[1]).T.astype(jnp.bfloat16)
    for head in range(HEADS):
        value_rows[head, :HEAD_DIM, :] = values[HEAD_DIM * head : HEAD_DIM * head + HEAD_DIM, :]
        value_rows[head, HEAD_DIM:, :] = jnp.ones((16, key_count), jnp.bfloat16)

    for pair in range(HEADS // 2):
        scores = dot_nt(key_pairs[pair], queries_ref[:, 128 * pair : 128 * pair + 128])
        for half in range(2):
            head = 2 * pair + half
            own = scores[half * key_count : half * key_count + key_count, :]
            powers = jnp.exp(own - jnp.max(own, axis=0, keepdims=True)).astype(jnp.bfloat16)
            blended = dot_nn(value_rows[head], powers)
            crossed[HEAD_DIM * head : HEAD_DIM * head + HEAD_DIM, :] = (
                blended[:HEAD_DIM, :] / blended[HEAD_DIM : HEAD_DIM + 1, :]
            ).astype(jnp.bfloat16)

    joined = dot_nn(w_back_ref[...], crossed[...]) + dot_nn(w_embed_ref[...], features_ref[...])
    centred = joined - jnp.sum(joined, axis=0, keepdims=True) * (1.0 / width)
    spread = jnp.sum(centred * centred, axis=0, keepdims=True) * (1.0 / width)
    gain = jnp.concatenate([gain_head_ref[...]] * (joined.shape[1] // 128), axis=1)
    head_in = (centred * lax.rsqrt(spread + 1e-05) * gain).astype(jnp.bfloat16)
    hidden = jax.nn.gelu(dot_nn(w_hidden_ref[...], head_in)).astype(jnp.bfloat16)
    sdf_ref[...] = dot_nn(w_sdf_ref[...], hidden)[:1, :]


def tail(
    first, near, far, out_near, out_far, latents, gain_cross, w_kv, queries, features, w_back,
    w_embed, gain_head, w_hidden, w_sdf,
):
    points, width = queries.shape
    keys = latents.shape[0]
    vmem = pl.BlockSpec(memory_space=pltpu.VMEM)
    return pl.pallas_call(
        tail_kernel,
        in_specs=[pl.BlockSpec(memory_space=pltpu.SMEM)] + [vmem] * 14,
        out_specs=(vmem, vmem),
        out_shape=(
            jax.ShapeDtypeStruct((16, width), jnp.bfloat16),
            jax.ShapeDtypeStruct((1, points), jnp.float32),
        ),
        scratch_shapes=[
            pltpu.VMEM((keys, width), jnp.bfloat16),
            pltpu.VMEM((HEADS // 2, 2 * keys, 128), jnp.bfloat16),
            pltpu.VMEM((HEADS, HEAD_DIM + 16, keys), jnp.bfloat16),
            pltpu.VMEM((width, points), jnp.bfloat16),
        ],
        compiler_params=pltpu.CompilerParams(vmem_limit_bytes=VMEM_LIMIT),
        name="tail",
    )(
        first, near, far, out_near, out_far, latents, gain_cross, w_kv, queries, features, w_back,
        w_embed, gain_head, w_hidden, w_sdf,
    )


def swap(values, bit, count):
    return lax.ppermute(values, "query", [(i, i ^ bit) for i in range(count)])


def after(values, *others):
    return lax.optimization_barrier((values, *others))[0]


def one_head_each(
    latents, gain_self, w_qkv, w_out, gain_cross, w_kv, w_embed, gain_point, w_query, w_back,
    gain_head, w_hidden, w_sdf, *, points, count,
):
    me = lax.axis_index("query")
    rows = latents.shape[0]
    core = jnp.reshape(me % 2, (1,))
    packed = pack(w_qkv, latents)
    received = lax.all_to_all(packed, "query", split_axis=0, concat_axis=0, tiled=True)

    numbers = me * points + jnp.arange(points, dtype=jnp.int32)
    features = feature_rows(numbers)
    features = jnp.pad(features, ((0, FEATURE_ROWS - features.shape[0]), (0, 0)))
    w_embed = jnp.pad(w_embed, ((0, FEATURE_ROWS - w_embed.shape[0]), (0, 0)))
    queries = point_queries(after(features, packed), w_embed, gain_point[None, :], w_query)
    back = after(w_back, packed).T
    embed = after(w_embed, packed).T
    gain = jnp.broadcast_to(after(gain_head, packed)[:, None], (gain_head.shape[0], 128))
    sdf_row = jnp.pad(after(w_sdf, packed)[None, :], ((0, 15), (0, 0)))
    out = w_out
    out = jnp.concatenate([out, swap(after(out, packed), 8, count)], axis=0)

    received, queries, back, embed, gain, sdf_row = lax.optimization_barrier(
        (received, queries, back, embed, gain, sdf_row)
    )
    own = unpack(received)
    other = swap(own, 1, count)
    out_swapped = swap(after(out, received), 4, count)
    attended, all_latents = self_attention(core, received, own, other, gain_self[None, :])

    hidden = after(w_hidden, attended).T
    attended = jnp.concatenate([attended, swap(attended, 8, count)], axis=0)
    out = jnp.concatenate([out, after(out_swapped, attended)], axis=0)
    out_swapped = swap(out, 2, count)
    attended = jnp.concatenate([attended, swap(attended, 4, count)], axis=0)
    attended = jnp.concatenate([attended, swap(attended, 2, count)], axis=0)
    out = jnp.concatenate([out, after(out_swapped, attended)], axis=0)
    far = swap(attended, 1, count)
    out_far = swap(out, 1, count)
    decoded, sdf = tail(
        jnp.reshape(me * rows, (1,)), attended, far, out, out_far, all_latents,
        gain_cross[None, :], w_kv, queries, features, back, embed, gain, hidden, sdf_row,
    )
    return decoded, sdf[0]


def solution(mesh):
    parts, count = mesh.shape["shape"], mesh.shape["query"]

    def program(latents, *others):
        own = latents.shape[0] // (parts * count)
        points = 1024
        shards = functools.partial(any_slice, points=points)
        if count == HEADS and own == 16 and others[1].shape[1] // count == 64:
            shards = functools.partial(one_head_each, points=points, count=count)
        return jax.shard_map(
            shards,
            mesh=mesh,
            in_specs=(
                P(("shape", "query"), None),
                P(),
                P(None, "query", None),
                P("query", None),
                P(),
                P(),
                P(),
                P(),
                P(),
                P(),
                P(),
                P(),
                P(),
            ),
            out_specs=(P(("shape", "query"), None), P(("shape", "query"))),
            check_vma=False,
        )(latents, *others)

    return program
```

```python
import functools
import math

import jax
import jax.numpy as jnp
from jax import lax
from jax.experimental import pallas as pl
from jax.experimental.pallas import tpu as pltpu
from jax.sharding import PartitionSpec as P

HEADS = 16
FREQS = 8
GRID = 512
HEAD_DIM = 64
SCALE = 1.0 / math.sqrt(HEAD_DIM)
POINT_BLOCK = 512
TAIL_LIMIT = 58
FEATURE_ROWS = 64
EXCHANGES = (8, 2, 4, 1)


def norm_rows(values, gain):
    center = jnp.mean(values, axis=-1, keepdims=True)
    centred = values - center
    spread = jnp.mean(centred * centred, axis=-1, keepdims=True)
    return centred * lax.rsqrt(spread + 1e-05) * gain


def attend(queries, keys, values):
    row_count, features = queries.shape
    key_count = keys.shape[0]
    head_dim = features // HEADS
    group_count = HEADS // 4
    head_queries = queries.reshape(row_count, group_count, 4, head_dim).transpose(1, 0, 2, 3)
    head_keys = keys.reshape(key_count, group_count, 4, head_dim).transpose(1, 0, 2, 3)
    head_values = values.reshape(key_count, group_count, 4, head_dim).transpose(1, 0, 2, 3)
    scaling = 1.0 / math.sqrt(head_dim)

    def per_group(block):
        group_query, group_keys, group_values = block
        scores = (
            jnp.einsum("rge,nge->grn", group_query, group_keys, preferred_element_type=jnp.float32)
            * scaling
        )
        highest = jnp.max(scores, axis=-1, keepdims=True)
        powers = jnp.exp(scores - highest)
        total = jnp.sum(powers, axis=-1, keepdims=True)
        weights = (powers / total).astype(jnp.bfloat16)
        blended = jnp.einsum(
            "grn,nge->rge", weights, group_values, preferred_element_type=jnp.float32
        )
        return blended.astype(jnp.bfloat16)

    result = lax.map(per_group, (head_queries, head_keys, head_values))
    return result.transpose(1, 0, 2, 3).reshape(row_count, features)


def feature_rows(numbers):
    cell_i = numbers // (GRID * GRID)
    cell_j = numbers // GRID % GRID
    cell_k = numbers % GRID
    cells = jnp.stack([cell_i, cell_j, cell_k], axis=0).astype(jnp.float32)
    coords = (2.0 * cells + 1.0) / GRID - 1.0
    freqs = 2.0 ** jnp.arange(FREQS, dtype=jnp.float32) * math.pi
    angles = (coords[:, None, :] * freqs[None, :, None]).reshape(3 * FREQS, numbers.shape[0])
    return jnp.concatenate([coords, jnp.sin(angles), jnp.cos(angles)], axis=0).astype(jnp.bfloat16)


def any_slice(
    latents, gain_self, w_qkv, w_out, gain_cross, w_kv, w_embed, gain_point, w_query, w_back,
    gain_head, w_hidden, w_sdf, *, points,
):
    inputs = latents.astype(jnp.float32)
    normed = norm_rows(inputs, gain_self).astype(jnp.bfloat16)
    qkv = jnp.einsum(
        "rd,sdc->src",
        normed,
        lax.all_gather(w_qkv, "query", axis=1, tiled=True),
        preferred_element_type=jnp.float32,
    ).astype(jnp.bfloat16)
    self_keys, self_values = (
        lax.all_gather(qkv[1], "query", axis=0, tiled=True),
        lax.all_gather(qkv[2], "query", axis=0, tiled=True),
    )
    attended = attend(qkv[0], self_keys, self_values)
    update = jnp.dot(
        attended,
        lax.all_gather(w_out, "query", axis=0, tiled=True),
        preferred_element_type=jnp.float32,
    )
    decoded = (inputs + update).astype(jnp.bfloat16)
    normed_two = norm_rows(decoded.astype(jnp.float32), gain_cross).astype(jnp.bfloat16)
    stacked = jnp.einsum(
        "rd,sdc->src",
        lax.all_gather(normed_two, "query", axis=0, tiled=True),
        w_kv,
        preferred_element_type=jnp.float32,
    ).astype(jnp.bfloat16)
    numbers = lax.axis_index("query") * points + jnp.arange(points, dtype=jnp.int32)
    features = feature_rows(numbers).T
    embedded = jnp.dot(features, w_embed, preferred_element_type=jnp.float32)
    point_normed = norm_rows(embedded, gain_point).astype(jnp.bfloat16)
    point_query = jnp.dot(point_normed, w_query, preferred_element_type=jnp.float32).astype(
        jnp.bfloat16
    )
    crossed = attend(point_query, stacked[0], stacked[1])
    joined = embedded + jnp.dot(crossed, w_back, preferred_element_type=jnp.float32)
    head_in = norm_rows(joined, gain_head).astype(jnp.bfloat16)
    hidden = jax.nn.gelu(jnp.dot(head_in, w_hidden, preferred_element_type=jnp.float32)).astype(
        jnp.bfloat16
    )
    sdf = jnp.dot(hidden, w_sdf, preferred_element_type=jnp.float32)
    return (decoded, sdf)


def dot_nn(left, right):
    return lax.dot_general(left, right, (((1,), (0,)), ((), ())), preferred_element_type=jnp.float32)


def dot_nt(left, right):
    return lax.dot_general(left, right, (((1,), (1,)), ((), ())), preferred_element_type=jnp.float32)


def dot_tn(left, right):
    return lax.dot_general(left, right, (((0,), (0,)), ((), ())), preferred_element_type=jnp.float32)


def limit(mebibytes):
    return pltpu.CompilerParams(vmem_limit_bytes=mebibytes * 1024 * 1024)


def pack_kernel(w_ref, latents_ref, out_ref):
    rows = w_ref.shape[1]
    count, width = latents_ref.shape
    pieces = width // 256
    for target in range(HEADS):
        low = target * HEAD_DIM
        query, key, value = (w_ref[s, :, low : low + HEAD_DIM] for s in range(3))
        out_ref[target, :rows, :] = jnp.concatenate([query, key], axis=1)
        out_ref[target, rows : rows + rows // 2, :] = jnp.concatenate(
            [value[: rows // 2], value[rows // 2 :]], axis=1
        )
        for piece in range(pieces):
            place = rows + rows // 2 + piece * count
            first = 128 * (piece + pieces * (target % 2))
            out_ref[target, place : place + count, :] = latents_ref[:, first : first + 128]


def pack(w_qkv, latents):
    rows = w_qkv.shape[1]
    count, width = latents.shape
    depth = rows + rows // 2 + count * (width // 256)
    return pl.pallas_call(
        pack_kernel,
        out_shape=jax.ShapeDtypeStruct((HEADS, depth, 128), jnp.bfloat16),
        name="pack",
    )(w_qkv, latents)


def unpack_kernel(received_ref, half_ref):
    rows, width = half_ref.shape
    count = rows // HEADS
    first = received_ref.shape[1] - count * (width // 128)
    for piece in range(width // 128):
        low = first + piece * count
        half_ref[:, 128 * piece : 128 * piece + 128] = received_ref[:, low : low + count, :].reshape(
            rows, 128
        )


def unpack(received, count, width):
    return pl.pallas_call(
        unpack_kernel,
        out_shape=jax.ShapeDtypeStruct((count * HEADS, width // 2), jnp.bfloat16),
        compiler_params=limit(4),
        name="unpack",
    )(received)


def point_norm_kernel(features_ref, w_embed_ref, gain_ref, out_ref):
    embedded = dot_tn(features_ref[...], w_embed_ref[...])
    out_ref[...] = norm_rows(embedded, gain_ref[...]).astype(jnp.bfloat16)


def point_norms(features, w_embed, gain):
    points, width = features.shape[1], w_embed.shape[1]
    return pl.pallas_call(
        point_norm_kernel,
        out_shape=jax.ShapeDtypeStruct((points, width), jnp.bfloat16),
        compiler_params=limit(16),
        cost_estimate=pl.CostEstimate(
            flops=16 * points * width, bytes_accessed=8 * points * width, transcendentals=0
        ),
        name="point_norms",
    )(features, w_embed, gain)


def point_query_kernel(normed_ref, w_query_ref, out_ref):
    out_ref[...] = dot_nn(normed_ref[...], w_query_ref[...]).astype(jnp.bfloat16)


def point_queries(normed, w_query):
    points, width = normed.shape
    return pl.pallas_call(
        point_query_kernel,
        grid=(points // POINT_BLOCK,),
        in_specs=[
            pl.BlockSpec((POINT_BLOCK, width), lambda i: (i, 0)),
            pl.BlockSpec((width, width), lambda i: (0, 0)),
        ],
        out_specs=pl.BlockSpec((POINT_BLOCK, width), lambda i: (i, 0)),
        out_shape=jax.ShapeDtypeStruct((points, width), jnp.bfloat16),
        cost_estimate=pl.CostEstimate(
            flops=2 * points * width * width, bytes_accessed=6 * width * width, transcendentals=0
        ),
        name="point_queries",
    )(normed, w_query)


def joined_halves(core, own, other):
    first = core == 0
    return jnp.concatenate([jnp.where(first, own, other), jnp.where(first, other, own)], axis=1)


def self_kernel(place_ref, received_ref, own_ref, other_ref, gain_ref, out_ref):
    latents = joined_halves(place_ref[1], own_ref[...], other_ref[...])
    normed = norm_rows(latents.astype(jnp.float32), gain_ref[...]).astype(jnp.bfloat16)
    width = latents.shape[1]
    rows = width // HEADS
    query_key = dot_nn(normed, received_ref[:, :rows, :].reshape(width, 2 * HEAD_DIM))
    query_key = query_key.astype(jnp.bfloat16)
    folded = received_ref[:, rows : rows + rows // 2, :]
    w_value = jnp.concatenate([folded[:, :, :HEAD_DIM], folded[:, :, HEAD_DIM:]], axis=1)
    values = dot_nn(normed, w_value.reshape(width, HEAD_DIM)).astype(jnp.bfloat16)
    scores = dot_nt(query_key[:, HEAD_DIM:], query_key[:, :HEAD_DIM]) * SCALE
    powers = jnp.exp(scores - jnp.max(scores, axis=0, keepdims=True))
    shares = (powers / jnp.sum(powers, axis=0, keepdims=True)).astype(jnp.bfloat16)
    attended = dot_tn(values, shares).astype(jnp.bfloat16)
    half = HEAD_DIM // 2
    for target in range(HEADS):
        out_ref[target] = attended[half * (target % 2) : half * (target % 2) + half, :]


def self_attention(place, received, own, other, gain):
    vmem = pl.BlockSpec(memory_space=pltpu.VMEM)
    return pl.pallas_call(
        self_kernel,
        in_specs=[pl.BlockSpec(memory_space=pltpu.SMEM)] + [vmem] * 4,
        out_shape=jax.ShapeDtypeStruct((HEADS, HEAD_DIM // 2, own.shape[0]), jnp.bfloat16),
        compiler_params=limit(8),
        name="self_attention",
    )(place, received, own, other, gain)


def tail_kernel(
    place_ref, near_ref, far_ref, out_0_ref, out_1_ref, out_2_ref, out_3_ref, own_ref, other_ref,
    gain_cross_ref, w_kv_ref,
    queries_ref, features_ref, w_back_ref, w_embed_ref, gain_head_ref, w_hidden_ref, w_sdf_ref,
    decoded_ref, sdf_ref, attended, all_decoded, key_pairs, value_rows, crossed,
    w_kv, queries, w_back, w_hidden, semaphores,
):
    loads = [
        pltpu.make_async_copy(source, target, semaphores.at[i])
        for i, (source, target) in enumerate(
            ((w_kv_ref, w_kv), (queries_ref, queries), (w_back_ref, w_back), (w_hidden_ref, w_hidden))
        )
    ]
    for load in loads:
        load.start()
    me, core = place_ref[0], place_ref[1]
    half = HEAD_DIM // 2
    for block in range(HEADS):
        head = me ^ sum(bit for place, bit in enumerate(EXCHANGES) if block >> place & 1)
        for side_ref, place in ((near_ref, core), (far_ref, 1 - core)):
            row = pl.multiple_of(HEAD_DIM * block + half * place, half)
            attended[pl.ds(row, half), :] = side_ref[head]
    update = joined_halves(core, own_ref[...], other_ref[...]).astype(jnp.float32)
    quarter = out_0_ref.shape[0]
    for piece, out_ref in enumerate((out_0_ref, out_1_ref, out_2_ref, out_3_ref)):
        update += dot_tn(attended[quarter * piece : quarter * piece + quarter, :], out_ref[...])
    decoded = update.astype(jnp.bfloat16)
    all_decoded[...] = decoded
    rows = decoded_ref.shape[0]
    decoded_ref[...] = all_decoded[pl.ds(pl.multiple_of(me * rows, rows), rows), :]
    normed = norm_rows(decoded.astype(jnp.float32), gain_cross_ref[...]).astype(jnp.bfloat16)
    loads[0].wait()
    keys = dot_nn(normed, w_kv[0]).astype(jnp.bfloat16) * SCALE
    key_count = keys.shape[0]
    lane = lax.broadcasted_iota(jnp.int32, (key_count, 128), 1)
    for pair in range(HEADS // 2):
        both = keys[:, 128 * pair : 128 * pair + 128]
        zero = jnp.zeros_like(both)
        key_pairs[pair, :key_count, :] = jnp.where(lane < HEAD_DIM, both, zero)
        key_pairs[pair, key_count:, :] = jnp.where(lane < HEAD_DIM, zero, both)
    values = dot_nn(normed, w_kv[1]).T.astype(jnp.bfloat16)
    for head in range(HEADS):
        value_rows[head, :HEAD_DIM, :] = values[HEAD_DIM * head : HEAD_DIM * head + HEAD_DIM, :]
        value_rows[head, HEAD_DIM:, :] = jnp.ones((16, key_count), jnp.bfloat16)

    loads[1].wait()
    for pair in range(HEADS // 2):
        scores = dot_nt(key_pairs[pair], queries[:, 128 * pair : 128 * pair + 128])
        for side in range(2):
            head = 2 * pair + side
            own = scores[side * key_count : side * key_count + key_count, :]
            powers = jnp.exp(own - jnp.max(own, axis=0, keepdims=True)).astype(jnp.bfloat16)
            blended = dot_nn(value_rows[head], powers)
            crossed[HEAD_DIM * head : HEAD_DIM * head + HEAD_DIM, :] = (
                blended[:HEAD_DIM, :] / blended[HEAD_DIM : HEAD_DIM + 1, :]
            ).astype(jnp.bfloat16)

    loads[2].wait()
    joined = dot_tn(crossed[...], w_back[...]) + dot_tn(features_ref[...], w_embed_ref[...])
    head_in = norm_rows(joined, gain_head_ref[...]).astype(jnp.bfloat16)
    loads[3].wait()
    hidden = jax.nn.gelu(dot_nn(head_in, w_hidden[...])).astype(jnp.bfloat16)
    sdf_ref[...] = dot_nt(w_sdf_ref[...], hidden)[:1, :]


def tail(
    place, near, far, outs, own, other, gain_cross, w_kv, queries, features, w_back, w_embed,
    gain_head, w_hidden, w_sdf,
):
    points, width = queries.shape
    keys = own.shape[0]
    hbm = pl.BlockSpec(memory_space=pl.ANY)
    vmem = pl.BlockSpec(memory_space=pltpu.VMEM)
    return pl.pallas_call(
        tail_kernel,
        in_specs=[pl.BlockSpec(memory_space=pltpu.SMEM)]
        + [vmem] * 9
        + [hbm, hbm, vmem, hbm, vmem, vmem, hbm, vmem],
        out_specs=(vmem, vmem),
        out_shape=(
            jax.ShapeDtypeStruct((keys // HEADS, width), jnp.bfloat16),
            jax.ShapeDtypeStruct((1, points), jnp.float32),
        ),
        scratch_shapes=[
            pltpu.VMEM((width, keys), jnp.bfloat16),
            pltpu.VMEM((keys, width), jnp.bfloat16),
            pltpu.VMEM((HEADS // 2, 2 * keys, 128), jnp.bfloat16),
            pltpu.VMEM((HEADS, HEAD_DIM + 16, keys), jnp.bfloat16),
            pltpu.VMEM((width, points), jnp.bfloat16),
            pltpu.VMEM(w_kv.shape, jnp.bfloat16),
            pltpu.VMEM(queries.shape, jnp.bfloat16),
            pltpu.VMEM(w_back.shape, jnp.bfloat16),
            pltpu.VMEM(w_hidden.shape, jnp.bfloat16),
            pltpu.SemaphoreType.DMA((4,)),
        ],
        compiler_params=limit(TAIL_LIMIT),
        name="tail",
    )(
        place, near, far, *outs, own, other, gain_cross, w_kv, queries, features, w_back, w_embed,
        gain_head, w_hidden, w_sdf,
    )


def swap(values, bit, count):
    return lax.ppermute(values, "query", [(i, i ^ bit) for i in range(count)])


def to_all(blocks):
    return lax.all_to_all(blocks, "query", split_axis=0, concat_axis=0, tiled=True)


def after(values, *others):
    return lax.optimization_barrier((values, *others))[0]


def one_head_each(
    latents, gain_self, w_qkv, w_out, gain_cross, w_kv, w_embed, gain_point, w_query, w_back,
    gain_head, w_hidden, w_sdf, *, points, count,
):
    me = lax.axis_index("query")
    place = jnp.stack([me, me & 1])
    received = to_all(pack(w_qkv, latents))

    numbers = me * points + jnp.arange(points, dtype=jnp.int32)
    features = feature_rows(numbers)
    features = jnp.pad(features, ((0, FEATURE_ROWS - features.shape[0]), (0, 0)))
    w_embed = jnp.pad(w_embed, ((0, FEATURE_ROWS - w_embed.shape[0]), (0, 0)))
    sdf_row = jnp.pad(w_sdf[None, :], ((0, 15), (0, 0)))
    out = jnp.concatenate([w_out, swap(w_out, EXCHANGES[0], count)], axis=0)
    out_swapped = swap(out, EXCHANGES[1], count)
    normed = point_norms(after(features, out), w_embed, gain_point[None, :])
    out_0 = jnp.concatenate([out, after(out_swapped, normed)], axis=0)
    out_1 = swap(out_0, EXCHANGES[2], count)
    queries = point_queries(normed, w_query)

    received, queries, features, w_embed, sdf_row, place = lax.optimization_barrier(
        (received, queries, features, w_embed, sdf_row, place)
    )
    own = unpack(received, latents.shape[0], latents.shape[1])
    other = swap(own, 1, count)
    out_2 = swap(after(out_0, own), EXCHANGES[3], count)
    attended = self_attention(place, received, own, other, gain_self[None, :])
    near = to_all(attended)
    out_3 = swap(after(out_1, near), EXCHANGES[3], count)
    far = swap(near, 1, count)
    decoded, sdf = tail(
        place, near, far, (out_0, out_1, out_2, out_3), own, other, gain_cross[None, :], w_kv,
        queries, features, w_back, w_embed, gain_head[None, :], w_hidden, sdf_row,
    )
    return decoded, sdf[0]


def solution(mesh):
    parts, count = mesh.shape["shape"], mesh.shape["query"]

    def program(latents, *others):
        own = latents.shape[0] // (parts * count)
        points = 1024
        shards = functools.partial(any_slice, points=points)
        if count == HEADS and own == 16 and others[1].shape[1] // count == 64:
            shards = functools.partial(one_head_each, points=points, count=count)
        return jax.shard_map(
            shards,
            mesh=mesh,
            in_specs=(
                P(("shape", "query"), None),
                P(),
                P(None, "query", None),
                P("query", None),
                P(),
                P(),
                P(),
                P(),
                P(),
                P(),
                P(),
                P(),
                P(),
            ),
            out_specs=(P(("shape", "query"), None), P(("shape", "query"))),
            check_vma=False,
        )(latents, *others)

    return program
```

```python
import functools
import math

import jax
import jax.numpy as jnp
from jax import lax
from jax.experimental import pallas as pl
from jax.experimental.pallas import tpu as pltpu
from jax.sharding import PartitionSpec as P

HEADS = 16
FREQS = 8
GRID = 512
HEAD_DIM = 64
SCALE = 1.0 / math.sqrt(HEAD_DIM)
POINT_BLOCK = 512
TAIL_LIMIT = 16
FEATURE_ROWS = 64
EXCHANGES = (8, 2, 4, 1)
HEAD_EXCHANGES = (2, 8, 4, 1)


def norm_rows(values, gain):
    center = jnp.mean(values, axis=-1, keepdims=True)
    centred = values - center
    spread = jnp.mean(centred * centred, axis=-1, keepdims=True)
    return centred * lax.rsqrt(spread + 1e-05) * gain


def attend(queries, keys, values):
    row_count, features = queries.shape
    key_count = keys.shape[0]
    head_dim = features // HEADS
    group_count = HEADS // 4
    head_queries = queries.reshape(row_count, group_count, 4, head_dim).transpose(1, 0, 2, 3)
    head_keys = keys.reshape(key_count, group_count, 4, head_dim).transpose(1, 0, 2, 3)
    head_values = values.reshape(key_count, group_count, 4, head_dim).transpose(1, 0, 2, 3)
    scaling = 1.0 / math.sqrt(head_dim)

    def per_group(block):
        group_query, group_keys, group_values = block
        scores = (
            jnp.einsum("rge,nge->grn", group_query, group_keys, preferred_element_type=jnp.float32)
            * scaling
        )
        highest = jnp.max(scores, axis=-1, keepdims=True)
        powers = jnp.exp(scores - highest)
        total = jnp.sum(powers, axis=-1, keepdims=True)
        weights = (powers / total).astype(jnp.bfloat16)
        blended = jnp.einsum(
            "grn,nge->rge", weights, group_values, preferred_element_type=jnp.float32
        )
        return blended.astype(jnp.bfloat16)

    result = lax.map(per_group, (head_queries, head_keys, head_values))
    return result.transpose(1, 0, 2, 3).reshape(row_count, features)


def feature_rows(numbers):
    cell_i = numbers // (GRID * GRID)
    cell_j = numbers // GRID % GRID
    cell_k = numbers % GRID
    cells = jnp.stack([cell_i, cell_j, cell_k], axis=0).astype(jnp.float32)
    coords = (2.0 * cells + 1.0) / GRID - 1.0
    freqs = 2.0 ** jnp.arange(FREQS, dtype=jnp.float32) * math.pi
    angles = (coords[:, None, :] * freqs[None, :, None]).reshape(3 * FREQS, numbers.shape[0])
    return jnp.concatenate([coords, jnp.sin(angles), jnp.cos(angles)], axis=0).astype(jnp.bfloat16)


def any_slice(
    latents, gain_self, w_qkv, w_out, gain_cross, w_kv, w_embed, gain_point, w_query, w_back,
    gain_head, w_hidden, w_sdf, *, points,
):
    inputs = latents.astype(jnp.float32)
    normed = norm_rows(inputs, gain_self).astype(jnp.bfloat16)
    qkv = jnp.einsum(
        "rd,sdc->src",
        normed,
        lax.all_gather(w_qkv, "query", axis=1, tiled=True),
        preferred_element_type=jnp.float32,
    ).astype(jnp.bfloat16)
    self_keys, self_values = (
        lax.all_gather(qkv[1], "query", axis=0, tiled=True),
        lax.all_gather(qkv[2], "query", axis=0, tiled=True),
    )
    attended = attend(qkv[0], self_keys, self_values)
    update = jnp.dot(
        attended,
        lax.all_gather(w_out, "query", axis=0, tiled=True),
        preferred_element_type=jnp.float32,
    )
    decoded = (inputs + update).astype(jnp.bfloat16)
    normed_two = norm_rows(decoded.astype(jnp.float32), gain_cross).astype(jnp.bfloat16)
    stacked = jnp.einsum(
        "rd,sdc->src",
        lax.all_gather(normed_two, "query", axis=0, tiled=True),
        w_kv,
        preferred_element_type=jnp.float32,
    ).astype(jnp.bfloat16)
    numbers = lax.axis_index("query") * points + jnp.arange(points, dtype=jnp.int32)
    features = feature_rows(numbers).T
    embedded = jnp.dot(features, w_embed, preferred_element_type=jnp.float32)
    point_normed = norm_rows(embedded, gain_point).astype(jnp.bfloat16)
    point_query = jnp.dot(point_normed, w_query, preferred_element_type=jnp.float32).astype(
        jnp.bfloat16
    )
    crossed = attend(point_query, stacked[0], stacked[1])
    joined = embedded + jnp.dot(crossed, w_back, preferred_element_type=jnp.float32)
    head_in = norm_rows(joined, gain_head).astype(jnp.bfloat16)
    hidden = jax.nn.gelu(jnp.dot(head_in, w_hidden, preferred_element_type=jnp.float32)).astype(
        jnp.bfloat16
    )
    sdf = jnp.dot(hidden, w_sdf, preferred_element_type=jnp.float32)
    return (decoded, sdf)


def dot_nn(left, right):
    return lax.dot_general(left, right, (((1,), (0,)), ((), ())), preferred_element_type=jnp.float32)


def dot_nt(left, right):
    return lax.dot_general(left, right, (((1,), (1,)), ((), ())), preferred_element_type=jnp.float32)


def dot_tn(left, right):
    return lax.dot_general(left, right, (((0,), (0,)), ((), ())), preferred_element_type=jnp.float32)


def limit(mebibytes):
    return pltpu.CompilerParams(vmem_limit_bytes=mebibytes * 1024 * 1024)


def pack_kernel(w_ref, latents_ref, out_ref):
    rows = w_ref.shape[1]
    count, width = latents_ref.shape
    pieces = width // 256
    for target in range(HEADS):
        low = target * HEAD_DIM
        query, key, value = (w_ref[s, :, low : low + HEAD_DIM] for s in range(3))
        out_ref[target, :rows, :] = jnp.concatenate([query, key], axis=1)
        out_ref[target, rows : rows + rows // 2, :] = jnp.concatenate(
            [value[: rows // 2], value[rows // 2 :]], axis=1
        )
        for piece in range(pieces):
            place = rows + rows // 2 + piece * count
            first = 128 * (piece + pieces * (target % 2))
            out_ref[target, place : place + count, :] = latents_ref[:, first : first + 128]


def pack(w_qkv, latents):
    rows = w_qkv.shape[1]
    count, width = latents.shape
    depth = rows + rows // 2 + count * (width // 256)
    return pl.pallas_call(
        pack_kernel,
        out_shape=jax.ShapeDtypeStruct((HEADS, depth, 128), jnp.bfloat16),
        name="pack",
    )(w_qkv, latents)


def unpack_kernel(received_ref, half_ref):
    rows, width = half_ref.shape
    count = rows // HEADS
    first = received_ref.shape[1] - count * (width // 128)
    for piece in range(width // 128):
        low = first + piece * count
        half_ref[:, 128 * piece : 128 * piece + 128] = received_ref[:, low : low + count, :].reshape(
            rows, 128
        )


def unpack(received, count, width):
    return pl.pallas_call(
        unpack_kernel,
        out_shape=jax.ShapeDtypeStruct((count * HEADS, width // 2), jnp.bfloat16),
        compiler_params=limit(4),
        cost_estimate=pl.CostEstimate(
            flops=2000000000, bytes_accessed=1024, transcendentals=0
        ),
        name="unpack",
    )(received)


def point_norm_kernel(features_ref, w_embed_ref, gain_ref, out_ref):
    embedded = dot_tn(features_ref[...], w_embed_ref[...])
    out_ref[...] = norm_rows(embedded, gain_ref[...]).astype(jnp.bfloat16)


def point_norms(features, w_embed, gain):
    points, width = features.shape[1], w_embed.shape[1]
    return pl.pallas_call(
        point_norm_kernel,
        out_shape=jax.ShapeDtypeStruct((points, width), jnp.bfloat16),
        compiler_params=limit(16),
        cost_estimate=pl.CostEstimate(flops=1024, bytes_accessed=1024, transcendentals=0),
        name="point_norms",
    )(features, w_embed, gain)


def point_query_kernel(normed_ref, w_query_ref, out_ref):
    out_ref[...] = dot_nn(normed_ref[...], w_query_ref[...]).astype(jnp.bfloat16)


def point_queries(normed, w_query):
    points, width = normed.shape
    return pl.pallas_call(
        point_query_kernel,
        grid=(points // POINT_BLOCK,),
        in_specs=[
            pl.BlockSpec((POINT_BLOCK, width), lambda i: (i, 0)),
            pl.BlockSpec((width, width), lambda i: (0, 0)),
        ],
        out_specs=pl.BlockSpec((POINT_BLOCK, width), lambda i: (i, 0)),
        out_shape=jax.ShapeDtypeStruct((points, width), jnp.bfloat16),
        cost_estimate=pl.CostEstimate(flops=1024, bytes_accessed=1024, transcendentals=0),
        name="point_queries",
    )(normed, w_query)


def joined_halves(core, own, other):
    first = core == 0
    return jnp.concatenate([jnp.where(first, own, other), jnp.where(first, other, own)], axis=1)


def self_kernel(place_ref, received_ref, own_ref, other_ref, gain_ref, out_ref):
    latents = joined_halves(place_ref[1], own_ref[...], other_ref[...])
    normed = norm_rows(latents.astype(jnp.float32), gain_ref[...]).astype(jnp.bfloat16)
    width = latents.shape[1]
    rows = width // HEADS
    query_key = dot_nn(normed, received_ref[:, :rows, :].reshape(width, 2 * HEAD_DIM))
    query_key = query_key.astype(jnp.bfloat16)
    folded = received_ref[:, rows : rows + rows // 2, :]
    w_value = jnp.concatenate([folded[:, :, :HEAD_DIM], folded[:, :, HEAD_DIM:]], axis=1)
    values = dot_nn(normed, w_value.reshape(width, HEAD_DIM)).astype(jnp.bfloat16)
    scores = dot_nt(query_key[:, HEAD_DIM:], query_key[:, :HEAD_DIM]) * SCALE
    powers = jnp.exp(scores - jnp.max(scores, axis=0, keepdims=True))
    shares = (powers / jnp.sum(powers, axis=0, keepdims=True)).astype(jnp.bfloat16)
    out_ref[...] = dot_tn(values, shares).astype(jnp.bfloat16)


def self_attention(place, received, own, other, gain):
    vmem = pl.BlockSpec(memory_space=pltpu.VMEM)
    return pl.pallas_call(
        self_kernel,
        in_specs=[pl.BlockSpec(memory_space=pltpu.SMEM)] + [vmem] * 4,
        out_shape=jax.ShapeDtypeStruct((HEAD_DIM, own.shape[0]), jnp.bfloat16),
        compiler_params=limit(8),
        name="self_attention",
    )(place, received, own, other, gain)


def tail_kernel(
    place_ref, near_ref, far_ref, out_0_ref, out_1_ref, out_2_ref, out_3_ref, own_ref, other_ref,
    gain_cross_ref, w_kv_ref,
    queries_ref, features_ref, w_back_ref, w_embed_ref, gain_head_ref, w_hidden_ref, w_sdf_ref,
    decoded_ref, sdf_ref, attended, all_decoded, key_pairs, value_rows, crossed,
):
    me, core = place_ref[0], place_ref[1]
    order = [EXCHANGES.index(bit) for bit in HEAD_EXCHANGES]
    for block in range(HEADS):
        place = sum(1 << to for at, to in enumerate(order) if block >> at & 1)
        side_ref = near_ref if block < HEADS // 2 else far_ref
        row = HEAD_DIM * (block % (HEADS // 2))
        attended[HEAD_DIM * place : HEAD_DIM * place + HEAD_DIM, :] = side_ref[
            row : row + HEAD_DIM, :
        ]
    update = joined_halves(core, own_ref[...], other_ref[...]).astype(jnp.float32)
    quarter = out_0_ref.shape[0]
    for piece, out_ref in enumerate((out_0_ref, out_1_ref, out_2_ref, out_3_ref)):
        update += dot_tn(attended[quarter * piece : quarter * piece + quarter, :], out_ref[...])
    decoded = update.astype(jnp.bfloat16)
    all_decoded[...] = decoded
    rows = decoded_ref.shape[0]
    decoded_ref[...] = all_decoded[pl.ds(pl.multiple_of(me * rows, rows), rows), :]
    normed = norm_rows(decoded.astype(jnp.float32), gain_cross_ref[...]).astype(jnp.bfloat16)
    keys = dot_nn(normed, w_kv_ref[0]).astype(jnp.bfloat16) * SCALE
    key_count = keys.shape[0]
    lane = lax.broadcasted_iota(jnp.int32, (key_count, 128), 1)
    for pair in range(HEADS // 2):
        both = keys[:, 128 * pair : 128 * pair + 128]
        zero = jnp.zeros_like(both)
        key_pairs[pair, :key_count, :] = jnp.where(lane < HEAD_DIM, both, zero)
        key_pairs[pair, key_count:, :] = jnp.where(lane < HEAD_DIM, zero, both)
    values = dot_nn(normed, w_kv_ref[1]).T.astype(jnp.bfloat16)
    for head in range(HEADS):
        value_rows[head, :HEAD_DIM, :] = values[HEAD_DIM * head : HEAD_DIM * head + HEAD_DIM, :]
        value_rows[head, HEAD_DIM:, :] = jnp.ones((16, key_count), jnp.bfloat16)

    for pair in range(HEADS // 2):
        scores = dot_nt(key_pairs[pair], queries_ref[:, 128 * pair : 128 * pair + 128])
        for side in range(2):
            head = 2 * pair + side
            own = scores[side * key_count : side * key_count + key_count, :]
            powers = jnp.exp(own - jnp.max(own, axis=0, keepdims=True)).astype(jnp.bfloat16)
            blended = dot_nn(value_rows[head], powers)
            crossed[HEAD_DIM * head : HEAD_DIM * head + HEAD_DIM, :] = (
                blended[:HEAD_DIM, :] / blended[HEAD_DIM : HEAD_DIM + 1, :]
            ).astype(jnp.bfloat16)

    joined = dot_tn(crossed[...], w_back_ref[...]) + dot_tn(features_ref[...], w_embed_ref[...])
    head_in = norm_rows(joined, gain_head_ref[...]).astype(jnp.bfloat16)
    hidden = jax.nn.gelu(dot_nn(head_in, w_hidden_ref[...])).astype(jnp.bfloat16)
    sdf_ref[...] = dot_nt(w_sdf_ref[...], hidden)[:1, :]


def tail(
    place, near, far, outs, own, other, gain_cross, w_kv, queries, features, w_back, w_embed,
    gain_head, w_hidden, w_sdf,
):
    points, width = queries.shape
    keys = own.shape[0]
    vmem = pl.BlockSpec(memory_space=pltpu.VMEM)
    return pl.pallas_call(
        tail_kernel,
        in_specs=[pl.BlockSpec(memory_space=pltpu.SMEM)]
        + [vmem] * 9
        + [vmem] * 8,
        out_specs=(vmem, vmem),
        out_shape=(
            jax.ShapeDtypeStruct((keys // HEADS, width), jnp.bfloat16),
            jax.ShapeDtypeStruct((1, points), jnp.float32),
        ),
        scratch_shapes=[
            pltpu.VMEM((width, keys), jnp.bfloat16),
            pltpu.VMEM((keys, width), jnp.bfloat16),
            pltpu.VMEM((HEADS // 2, 2 * keys, 128), jnp.bfloat16),
            pltpu.VMEM((HEADS, HEAD_DIM + 16, keys), jnp.bfloat16),
            pltpu.VMEM((width, points), jnp.bfloat16),
        ],
        compiler_params=limit(TAIL_LIMIT),
        name="tail",
    )(
        place, near, far, *outs, own, other, gain_cross, w_kv, queries, features, w_back, w_embed,
        gain_head, w_hidden, w_sdf,
    )


def swap(values, bit, count):
    return lax.ppermute(values, "query", [(i, i ^ bit) for i in range(count)])


def to_all(blocks):
    return lax.all_to_all(blocks, "query", split_axis=0, concat_axis=0, tiled=True)


def after(values, *others):
    return lax.optimization_barrier((values, *others))[0]


def one_head_each(
    latents, gain_self, w_qkv, w_out, gain_cross, w_kv, w_embed, gain_point, w_query, w_back,
    gain_head, w_hidden, w_sdf, *, points, count,
):
    me = lax.axis_index("query")
    place = jnp.stack([me, me & 1])
    received = to_all(pack(w_qkv, latents))

    numbers = me * points + jnp.arange(points, dtype=jnp.int32)
    features = feature_rows(numbers)
    features = jnp.pad(features, ((0, FEATURE_ROWS - features.shape[0]), (0, 0)))
    w_embed = jnp.pad(w_embed, ((0, FEATURE_ROWS - w_embed.shape[0]), (0, 0)))
    sdf_row = jnp.pad(w_sdf[None, :], ((0, 15), (0, 0)))
    out = jnp.concatenate([w_out, swap(w_out, EXCHANGES[0], count)], axis=0)
    out_swapped = swap(out, EXCHANGES[1], count)
    normed = point_norms(after(features, out), w_embed, gain_point[None, :])
    queries = point_queries(normed, w_query)
    out_0 = jnp.concatenate([out, after(out_swapped, queries)], axis=0)
    out_1 = swap(out_0, EXCHANGES[2], count)

    received, queries, features, w_embed, sdf_row, place, out_0 = lax.optimization_barrier(
        (received, queries, features, w_embed, sdf_row, place, out_0)
    )
    own = unpack(received, latents.shape[0], latents.shape[1])
    other = swap(own, 1, count)
    out_2 = swap(after(out_0, own), EXCHANGES[3], count)
    attended = self_attention(place, received, own, other, gain_self[None, :])
    near = attended
    for bit in HEAD_EXCHANGES[:3]:
        near = jnp.concatenate([near, swap(near, bit, count)], axis=0)
    out_3 = swap(out_1, EXCHANGES[3], count)
    far = swap(near, HEAD_EXCHANGES[3], count)
    decoded, sdf = tail(
        place, near, far, (out_0, out_1, out_2, out_3), own, other, gain_cross[None, :], w_kv,
        queries, features, w_back, w_embed, gain_head[None, :], w_hidden, sdf_row,
    )
    return decoded, sdf[0]


def solution(mesh):
    parts, count = mesh.shape["shape"], mesh.shape["query"]

    def program(latents, *others):
        own = latents.shape[0] // (parts * count)
        points = 1024
        shards = functools.partial(any_slice, points=points)
        if count == HEADS and own == 16 and others[1].shape[1] // count == 64:
            shards = functools.partial(one_head_each, points=points, count=count)
        return jax.shard_map(
            shards,
            mesh=mesh,
            in_specs=(
                P(("shape", "query"), None),
                P(),
                P(None, "query", None),
                P("query", None),
                P(),
                P(),
                P(),
                P(),
                P(),
                P(),
                P(),
                P(),
                P(),
            ),
            out_specs=(P(("shape", "query"), None), P(("shape", "query"))),
            check_vma=False,
        )(latents, *others)

    return program
```

```python
import functools
import math

import jax
import jax.numpy as jnp
from jax import lax
from jax.experimental import pallas as pl
from jax.experimental.pallas import tpu as pltpu
from jax.sharding import PartitionSpec as P

HEADS = 16
FREQS = 8
GRID = 512
HEAD_DIM = 64
SCALE = 1.0 / math.sqrt(HEAD_DIM)
POINT_BLOCK = 512
TAIL_LIMIT = 16
FEATURE_ROWS = 64
EXCHANGES = (8, 2, 4, 1)
HEAD_EXCHANGES = (2, 8, 4, 1)


def norm_rows(values, gain):
    center = jnp.mean(values, axis=-1, keepdims=True)
    centred = values - center
    spread = jnp.mean(centred * centred, axis=-1, keepdims=True)
    return centred * lax.rsqrt(spread + 1e-05) * gain


def attend(queries, keys, values):
    row_count, features = queries.shape
    key_count = keys.shape[0]
    head_dim = features // HEADS
    group_count = HEADS // 4
    head_queries = queries.reshape(row_count, group_count, 4, head_dim).transpose(1, 0, 2, 3)
    head_keys = keys.reshape(key_count, group_count, 4, head_dim).transpose(1, 0, 2, 3)
    head_values = values.reshape(key_count, group_count, 4, head_dim).transpose(1, 0, 2, 3)
    scaling = 1.0 / math.sqrt(head_dim)

    def per_group(block):
        group_query, group_keys, group_values = block
        scores = (
            jnp.einsum("rge,nge->grn", group_query, group_keys, preferred_element_type=jnp.float32)
            * scaling
        )
        highest = jnp.max(scores, axis=-1, keepdims=True)
        powers = jnp.exp(scores - highest)
        total = jnp.sum(powers, axis=-1, keepdims=True)
        weights = (powers / total).astype(jnp.bfloat16)
        blended = jnp.einsum(
            "grn,nge->rge", weights, group_values, preferred_element_type=jnp.float32
        )
        return blended.astype(jnp.bfloat16)

    result = lax.map(per_group, (head_queries, head_keys, head_values))
    return result.transpose(1, 0, 2, 3).reshape(row_count, features)


def feature_rows(numbers):
    cell_i = numbers // (GRID * GRID)
    cell_j = numbers // GRID % GRID
    cell_k = numbers % GRID
    cells = jnp.stack([cell_i, cell_j, cell_k], axis=0).astype(jnp.float32)
    coords = (2.0 * cells + 1.0) / GRID - 1.0
    freqs = 2.0 ** jnp.arange(FREQS, dtype=jnp.float32) * math.pi
    angles = (coords[:, None, :] * freqs[None, :, None]).reshape(3 * FREQS, numbers.shape[0])
    return jnp.concatenate([coords, jnp.sin(angles), jnp.cos(angles)], axis=0).astype(jnp.bfloat16)


def any_slice(
    latents, gain_self, w_qkv, w_out, gain_cross, w_kv, w_embed, gain_point, w_query, w_back,
    gain_head, w_hidden, w_sdf, *, points,
):
    inputs = latents.astype(jnp.float32)
    normed = norm_rows(inputs, gain_self).astype(jnp.bfloat16)
    qkv = jnp.einsum(
        "rd,sdc->src",
        normed,
        lax.all_gather(w_qkv, "query", axis=1, tiled=True),
        preferred_element_type=jnp.float32,
    ).astype(jnp.bfloat16)
    self_keys, self_values = (
        lax.all_gather(qkv[1], "query", axis=0, tiled=True),
        lax.all_gather(qkv[2], "query", axis=0, tiled=True),
    )
    attended = attend(qkv[0], self_keys, self_values)
    update = jnp.dot(
        attended,
        lax.all_gather(w_out, "query", axis=0, tiled=True),
        preferred_element_type=jnp.float32,
    )
    decoded = (inputs + update).astype(jnp.bfloat16)
    normed_two = norm_rows(decoded.astype(jnp.float32), gain_cross).astype(jnp.bfloat16)
    stacked = jnp.einsum(
        "rd,sdc->src",
        lax.all_gather(normed_two, "query", axis=0, tiled=True),
        w_kv,
        preferred_element_type=jnp.float32,
    ).astype(jnp.bfloat16)
    numbers = lax.axis_index("query") * points + jnp.arange(points, dtype=jnp.int32)
    features = feature_rows(numbers).T
    embedded = jnp.dot(features, w_embed, preferred_element_type=jnp.float32)
    point_normed = norm_rows(embedded, gain_point).astype(jnp.bfloat16)
    point_query = jnp.dot(point_normed, w_query, preferred_element_type=jnp.float32).astype(
        jnp.bfloat16
    )
    crossed = attend(point_query, stacked[0], stacked[1])
    joined = embedded + jnp.dot(crossed, w_back, preferred_element_type=jnp.float32)
    head_in = norm_rows(joined, gain_head).astype(jnp.bfloat16)
    hidden = jax.nn.gelu(jnp.dot(head_in, w_hidden, preferred_element_type=jnp.float32)).astype(
        jnp.bfloat16
    )
    sdf = jnp.dot(hidden, w_sdf, preferred_element_type=jnp.float32)
    return (decoded, sdf)


def dot_nn(left, right):
    return lax.dot_general(left, right, (((1,), (0,)), ((), ())), preferred_element_type=jnp.float32)


def dot_nt(left, right):
    return lax.dot_general(left, right, (((1,), (1,)), ((), ())), preferred_element_type=jnp.float32)


def dot_tn(left, right):
    return lax.dot_general(left, right, (((0,), (0,)), ((), ())), preferred_element_type=jnp.float32)


def limit(mebibytes):
    return pltpu.CompilerParams(vmem_limit_bytes=mebibytes * 1024 * 1024)


def pack_kernel(w_ref, latents_ref, out_ref):
    rows = w_ref.shape[1]
    count, width = latents_ref.shape
    pieces = width // 256
    for target in range(HEADS):
        low = target * HEAD_DIM
        query, key, value = (w_ref[s, :, low : low + HEAD_DIM] for s in range(3))
        out_ref[target, :rows, :] = jnp.concatenate([query, key], axis=1)
        out_ref[target, rows : rows + rows // 2, :] = jnp.concatenate(
            [value[: rows // 2], value[rows // 2 :]], axis=1
        )
        for piece in range(pieces):
            place = rows + rows // 2 + piece * count
            first = 128 * (piece + pieces * (target % 2))
            out_ref[target, place : place + count, :] = latents_ref[:, first : first + 128]


def pack(w_qkv, latents):
    rows = w_qkv.shape[1]
    count, width = latents.shape
    depth = rows + rows // 2 + count * (width // 256)
    return pl.pallas_call(
        pack_kernel,
        out_shape=jax.ShapeDtypeStruct((HEADS, depth, 128), jnp.bfloat16),
        name="pack",
    )(w_qkv, latents)


def unpack_kernel(received_ref, half_ref):
    rows, width = half_ref.shape
    count = rows // HEADS
    first = received_ref.shape[1] - count * (width // 128)
    for piece in range(width // 128):
        low = first + piece * count
        half_ref[:, 128 * piece : 128 * piece + 128] = received_ref[:, low : low + count, :].reshape(
            rows, 128
        )


def unpack(received, count, width):
    return pl.pallas_call(
        unpack_kernel,
        out_shape=jax.ShapeDtypeStruct((count * HEADS, width // 2), jnp.bfloat16),
        compiler_params=limit(4),
        cost_estimate=pl.CostEstimate(
            flops=2000000000, bytes_accessed=1024, transcendentals=0
        ),
        name="unpack",
    )(received)


def point_norm_kernel(features_ref, w_embed_ref, gain_ref, out_ref):
    embedded = dot_tn(features_ref[...], w_embed_ref[...])
    out_ref[...] = norm_rows(embedded, gain_ref[...]).astype(jnp.bfloat16)


def point_norms(features, w_embed, gain):
    points, width = features.shape[1], w_embed.shape[1]
    return pl.pallas_call(
        point_norm_kernel,
        out_shape=jax.ShapeDtypeStruct((points, width), jnp.bfloat16),
        compiler_params=limit(16),
        cost_estimate=pl.CostEstimate(flops=1024, bytes_accessed=1024, transcendentals=0),
        name="point_norms",
    )(features, w_embed, gain)


def point_query_kernel(normed_ref, w_query_ref, out_ref):
    out_ref[...] = dot_nn(normed_ref[...], w_query_ref[...]).astype(jnp.bfloat16)


def point_queries(normed, w_query):
    points, width = normed.shape
    return pl.pallas_call(
        point_query_kernel,
        grid=(points // POINT_BLOCK,),
        in_specs=[
            pl.BlockSpec((POINT_BLOCK, width), lambda i: (i, 0)),
            pl.BlockSpec((width, width), lambda i: (0, 0)),
        ],
        out_specs=pl.BlockSpec((POINT_BLOCK, width), lambda i: (i, 0)),
        out_shape=jax.ShapeDtypeStruct((points, width), jnp.bfloat16),
        cost_estimate=pl.CostEstimate(flops=1024, bytes_accessed=1024, transcendentals=0),
        name="point_queries",
    )(normed, w_query)


def joined_halves(core, own, other):
    first = core == 0
    return jnp.concatenate([jnp.where(first, own, other), jnp.where(first, other, own)], axis=1)


def self_kernel(place_ref, received_ref, own_ref, other_ref, gain_ref, out_ref):
    latents = joined_halves(place_ref[1], own_ref[...], other_ref[...])
    normed = norm_rows(latents.astype(jnp.float32), gain_ref[...]).astype(jnp.bfloat16)
    width = latents.shape[1]
    rows = width // HEADS
    query_key = dot_nn(normed, received_ref[:, :rows, :].reshape(width, 2 * HEAD_DIM))
    query_key = query_key.astype(jnp.bfloat16)
    folded = received_ref[:, rows : rows + rows // 2, :]
    w_value = jnp.concatenate([folded[:, :, :HEAD_DIM], folded[:, :, HEAD_DIM:]], axis=1)
    values = dot_nn(normed, w_value.reshape(width, HEAD_DIM)).astype(jnp.bfloat16)
    scores = dot_nt(query_key[:, HEAD_DIM:], query_key[:, :HEAD_DIM]) * SCALE
    powers = jnp.exp(scores - jnp.max(scores, axis=0, keepdims=True))
    shares = (powers / jnp.sum(powers, axis=0, keepdims=True)).astype(jnp.bfloat16)
    out_ref[...] = dot_tn(values, shares).astype(jnp.bfloat16)


def self_attention(place, received, own, other, gain):
    vmem = pl.BlockSpec(memory_space=pltpu.VMEM)
    return pl.pallas_call(
        self_kernel,
        in_specs=[pl.BlockSpec(memory_space=pltpu.SMEM)] + [vmem] * 4,
        out_shape=jax.ShapeDtypeStruct((HEAD_DIM, own.shape[0]), jnp.bfloat16),
        compiler_params=limit(8),
        name="self_attention",
    )(place, received, own, other, gain)


def tail_kernel(
    place_ref, near_ref, far_ref, out_0_ref, out_1_ref, out_2_ref, out_3_ref, own_ref, other_ref,
    gain_cross_ref, w_kv_ref,
    queries_ref, features_ref, w_back_ref, w_embed_ref, gain_head_ref, w_hidden_ref, w_sdf_ref,
    decoded_ref, sdf_ref, attended, all_decoded, key_pairs, value_rows, crossed,
):
    me, core = place_ref[0], place_ref[1]
    order = [EXCHANGES.index(bit) for bit in HEAD_EXCHANGES]
    for block in range(HEADS):
        place = sum(1 << to for at, to in enumerate(order) if block >> at & 1)
        side_ref = near_ref if block < HEADS // 2 else far_ref
        row = HEAD_DIM * (block % (HEADS // 2))
        attended[HEAD_DIM * place : HEAD_DIM * place + HEAD_DIM, :] = side_ref[
            row : row + HEAD_DIM, :
        ]
    update = joined_halves(core, own_ref[...], other_ref[...]).astype(jnp.float32)
    quarter = out_0_ref.shape[0]
    for piece, out_ref in enumerate((out_0_ref, out_1_ref, out_2_ref, out_3_ref)):
        update += dot_tn(attended[quarter * piece : quarter * piece + quarter, :], out_ref[...])
    decoded = update.astype(jnp.bfloat16)
    all_decoded[...] = decoded
    rows = decoded_ref.shape[0]
    decoded_ref[...] = all_decoded[pl.ds(pl.multiple_of(me * rows, rows), rows), :]
    normed = norm_rows(decoded.astype(jnp.float32), gain_cross_ref[...]).astype(jnp.bfloat16)
    keys = dot_nn(normed, w_kv_ref[0]).astype(jnp.bfloat16) * SCALE
    key_count = keys.shape[0]
    lane = lax.broadcasted_iota(jnp.int32, (key_count, 128), 1)
    for pair in range(HEADS // 2):
        both = keys[:, 128 * pair : 128 * pair + 128]
        zero = jnp.zeros_like(both)
        key_pairs[pair, :key_count, :] = jnp.where(lane < HEAD_DIM, both, zero)
        key_pairs[pair, key_count:, :] = jnp.where(lane < HEAD_DIM, zero, both)
    values = lax.dot_general(
        w_kv_ref[1], normed, (((0,), (1,)), ((), ())), preferred_element_type=jnp.float32
    ).astype(jnp.bfloat16)
    for head in range(HEADS):
        value_rows[head, :HEAD_DIM, :] = values[HEAD_DIM * head : HEAD_DIM * head + HEAD_DIM, :]
        value_rows[head, HEAD_DIM:, :] = jnp.ones((16, key_count), jnp.bfloat16)

    for pair in range(HEADS // 2):
        scores = dot_nt(key_pairs[pair], queries_ref[:, 128 * pair : 128 * pair + 128])
        for side in range(2):
            head = 2 * pair + side
            own = scores[side * key_count : side * key_count + key_count, :]
            powers = jnp.exp(own - jnp.max(own, axis=0, keepdims=True)).astype(jnp.bfloat16)
            blended = dot_nn(value_rows[head], powers)
            crossed[HEAD_DIM * head : HEAD_DIM * head + HEAD_DIM, :] = (
                blended[:HEAD_DIM, :] / blended[HEAD_DIM : HEAD_DIM + 1, :]
            ).astype(jnp.bfloat16)

    joined = dot_tn(crossed[...], w_back_ref[...]) + dot_tn(features_ref[...], w_embed_ref[...])
    head_in = norm_rows(joined, gain_head_ref[...]).astype(jnp.bfloat16)
    hidden = jax.nn.gelu(dot_nn(head_in, w_hidden_ref[...])).astype(jnp.bfloat16)
    sdf_ref[...] = dot_nt(w_sdf_ref[...], hidden)[:1, :]


def tail(
    place, near, far, outs, own, other, gain_cross, w_kv, queries, features, w_back, w_embed,
    gain_head, w_hidden, w_sdf,
):
    points, width = queries.shape
    keys = own.shape[0]
    vmem = pl.BlockSpec(memory_space=pltpu.VMEM)
    return pl.pallas_call(
        tail_kernel,
        in_specs=[pl.BlockSpec(memory_space=pltpu.SMEM)]
        + [vmem] * 9
        + [vmem] * 8,
        out_specs=(vmem, vmem),
        out_shape=(
            jax.ShapeDtypeStruct((keys // HEADS, width), jnp.bfloat16),
            jax.ShapeDtypeStruct((1, points), jnp.float32),
        ),
        scratch_shapes=[
            pltpu.VMEM((width, keys), jnp.bfloat16),
            pltpu.VMEM((keys, width), jnp.bfloat16),
            pltpu.VMEM((HEADS // 2, 2 * keys, 128), jnp.bfloat16),
            pltpu.VMEM((HEADS, HEAD_DIM + 16, keys), jnp.bfloat16),
            pltpu.VMEM((width, points), jnp.bfloat16),
        ],
        compiler_params=limit(TAIL_LIMIT),
        name="tail",
    )(
        place, near, far, *outs, own, other, gain_cross, w_kv, queries, features, w_back, w_embed,
        gain_head, w_hidden, w_sdf,
    )


def swap(values, bit, count):
    return lax.ppermute(values, "query", [(i, i ^ bit) for i in range(count)])


def to_all(blocks):
    return lax.all_to_all(blocks, "query", split_axis=0, concat_axis=0, tiled=True)


def after(values, *others):
    return lax.optimization_barrier((values, *others))[0]


def one_head_each(
    latents, gain_self, w_qkv, w_out, gain_cross, w_kv, w_embed, gain_point, w_query, w_back,
    gain_head, w_hidden, w_sdf, *, points, count,
):
    me = lax.axis_index("query")
    place = jnp.stack([me, me & 1])
    received = to_all(pack(w_qkv, latents))

    numbers = me * points + jnp.arange(points, dtype=jnp.int32)
    features = feature_rows(numbers)
    features = jnp.pad(features, ((0, FEATURE_ROWS - features.shape[0]), (0, 0)))
    w_embed = jnp.pad(w_embed, ((0, FEATURE_ROWS - w_embed.shape[0]), (0, 0)))
    sdf_row = jnp.pad(w_sdf[None, :], ((0, 15), (0, 0)))
    out = jnp.concatenate([w_out, swap(w_out, EXCHANGES[0], count)], axis=0)
    out_swapped = swap(out, EXCHANGES[1], count)
    normed = point_norms(after(features, out), w_embed, gain_point[None, :])
    queries = point_queries(normed, w_query)
    out_0 = jnp.concatenate([out, after(out_swapped, queries)], axis=0)
    out_1 = swap(out_0, EXCHANGES[2], count)

    received, queries, features, w_embed, sdf_row, place, out_0 = lax.optimization_barrier(
        (received, queries, features, w_embed, sdf_row, place, out_0)
    )
    own = unpack(received, latents.shape[0], latents.shape[1])
    other = swap(own, 1, count)
    out_2 = swap(after(out_0, own), EXCHANGES[3], count)
    attended = self_attention(place, received, own, other, gain_self[None, :])
    near = attended
    for bit in HEAD_EXCHANGES[:3]:
        near = jnp.concatenate([near, swap(near, bit, count)], axis=0)
    out_3 = swap(out_1, EXCHANGES[3], count)
    far = swap(near, HEAD_EXCHANGES[3], count)
    decoded, sdf = tail(
        place, near, far, (out_0, out_1, out_2, out_3), own, other, gain_cross[None, :], w_kv,
        queries, features, w_back, w_embed, gain_head[None, :], w_hidden, sdf_row,
    )
    return decoded, sdf[0]


def solution(mesh):
    parts, count = mesh.shape["shape"], mesh.shape["query"]

    def program(latents, *others):
        own = latents.shape[0] // (parts * count)
        points = 1024
        shards = functools.partial(any_slice, points=points)
        if count == HEADS and own == 16 and others[1].shape[1] // count == 64:
            shards = functools.partial(one_head_each, points=points, count=count)
        return jax.shard_map(
            shards,
            mesh=mesh,
            in_specs=(
                P(("shape", "query"), None),
                P(),
                P(None, "query", None),
                P("query", None),
                P(),
                P(),
                P(),
                P(),
                P(),
                P(),
                P(),
                P(),
                P(),
            ),
            out_specs=(P(("shape", "query"), None), P(("shape", "query"))),
            check_vma=False,
        )(latents, *others)

    return program
```

```python
import functools
import math

import jax
import jax.numpy as jnp
from jax import lax
from jax.experimental import pallas as pl
from jax.experimental.pallas import tpu as pltpu
from jax.sharding import PartitionSpec as P

HEADS = 16
FREQS = 8
GRID = 512
HEAD_DIM = 64
SCALE = 1.0 / math.sqrt(HEAD_DIM)
POINT_BLOCK = 512
TAIL_LIMIT = 16
FEATURE_ROWS = 64
EXCHANGES = (8, 2, 4, 1)
HEAD_EXCHANGES = (2, 8, 4, 1)


def norm_rows(values, gain):
    center = jnp.mean(values, axis=-1, keepdims=True)
    centred = values - center
    spread = jnp.mean(centred * centred, axis=-1, keepdims=True)
    return centred * lax.rsqrt(spread + 1e-05) * gain


def attend(queries, keys, values):
    row_count, features = queries.shape
    key_count = keys.shape[0]
    head_dim = features // HEADS
    group_count = HEADS // 4
    head_queries = queries.reshape(row_count, group_count, 4, head_dim).transpose(1, 0, 2, 3)
    head_keys = keys.reshape(key_count, group_count, 4, head_dim).transpose(1, 0, 2, 3)
    head_values = values.reshape(key_count, group_count, 4, head_dim).transpose(1, 0, 2, 3)
    scaling = 1.0 / math.sqrt(head_dim)

    def per_group(block):
        group_query, group_keys, group_values = block
        scores = (
            jnp.einsum("rge,nge->grn", group_query, group_keys, preferred_element_type=jnp.float32)
            * scaling
        )
        highest = jnp.max(scores, axis=-1, keepdims=True)
        powers = jnp.exp(scores - highest)
        total = jnp.sum(powers, axis=-1, keepdims=True)
        weights = (powers / total).astype(jnp.bfloat16)
        blended = jnp.einsum(
            "grn,nge->rge", weights, group_values, preferred_element_type=jnp.float32
        )
        return blended.astype(jnp.bfloat16)

    result = lax.map(per_group, (head_queries, head_keys, head_values))
    return result.transpose(1, 0, 2, 3).reshape(row_count, features)


def feature_rows(numbers):
    cell_i = numbers // (GRID * GRID)
    cell_j = numbers // GRID % GRID
    cell_k = numbers % GRID
    cells = jnp.stack([cell_i, cell_j, cell_k], axis=0).astype(jnp.float32)
    coords = (2.0 * cells + 1.0) / GRID - 1.0
    freqs = 2.0 ** jnp.arange(FREQS, dtype=jnp.float32) * math.pi
    angles = (coords[:, None, :] * freqs[None, :, None]).reshape(3 * FREQS, numbers.shape[0])
    return jnp.concatenate([coords, jnp.sin(angles), jnp.cos(angles)], axis=0).astype(jnp.bfloat16)


def any_slice(
    latents, gain_self, w_qkv, w_out, gain_cross, w_kv, w_embed, gain_point, w_query, w_back,
    gain_head, w_hidden, w_sdf, *, points,
):
    inputs = latents.astype(jnp.float32)
    normed = norm_rows(inputs, gain_self).astype(jnp.bfloat16)
    qkv = jnp.einsum(
        "rd,sdc->src",
        normed,
        lax.all_gather(w_qkv, "query", axis=1, tiled=True),
        preferred_element_type=jnp.float32,
    ).astype(jnp.bfloat16)
    self_keys, self_values = (
        lax.all_gather(qkv[1], "query", axis=0, tiled=True),
        lax.all_gather(qkv[2], "query", axis=0, tiled=True),
    )
    attended = attend(qkv[0], self_keys, self_values)
    update = jnp.dot(
        attended,
        lax.all_gather(w_out, "query", axis=0, tiled=True),
        preferred_element_type=jnp.float32,
    )
    decoded = (inputs + update).astype(jnp.bfloat16)
    normed_two = norm_rows(decoded.astype(jnp.float32), gain_cross).astype(jnp.bfloat16)
    stacked = jnp.einsum(
        "rd,sdc->src",
        lax.all_gather(normed_two, "query", axis=0, tiled=True),
        w_kv,
        preferred_element_type=jnp.float32,
    ).astype(jnp.bfloat16)
    numbers = lax.axis_index("query") * points + jnp.arange(points, dtype=jnp.int32)
    features = feature_rows(numbers).T
    embedded = jnp.dot(features, w_embed, preferred_element_type=jnp.float32)
    point_normed = norm_rows(embedded, gain_point).astype(jnp.bfloat16)
    point_query = jnp.dot(point_normed, w_query, preferred_element_type=jnp.float32).astype(
        jnp.bfloat16
    )
    crossed = attend(point_query, stacked[0], stacked[1])
    joined = embedded + jnp.dot(crossed, w_back, preferred_element_type=jnp.float32)
    head_in = norm_rows(joined, gain_head).astype(jnp.bfloat16)
    hidden = jax.nn.gelu(jnp.dot(head_in, w_hidden, preferred_element_type=jnp.float32)).astype(
        jnp.bfloat16
    )
    sdf = jnp.dot(hidden, w_sdf, preferred_element_type=jnp.float32)
    return (decoded, sdf)


def dot_nn(left, right):
    return lax.dot_general(left, right, (((1,), (0,)), ((), ())), preferred_element_type=jnp.float32)


def dot_nt(left, right):
    return lax.dot_general(left, right, (((1,), (1,)), ((), ())), preferred_element_type=jnp.float32)


def dot_tn(left, right):
    return lax.dot_general(left, right, (((0,), (0,)), ((), ())), preferred_element_type=jnp.float32)


def limit(mebibytes):
    return pltpu.CompilerParams(vmem_limit_bytes=mebibytes * 1024 * 1024)


def pack_kernel(w_ref, latents_ref, out_ref):
    rows = w_ref.shape[1]
    count, width = latents_ref.shape
    pieces = width // 256
    for target in range(HEADS):
        low = target * HEAD_DIM
        query, key, value = (w_ref[s, :, low : low + HEAD_DIM] for s in range(3))
        out_ref[target, :rows, :] = jnp.concatenate([query, key], axis=1)
        out_ref[target, rows : rows + rows // 2, :] = jnp.concatenate(
            [value[: rows // 2], value[rows // 2 :]], axis=1
        )
        for piece in range(pieces):
            place = rows + rows // 2 + piece * count
            first = 128 * (piece + pieces * (target % 2))
            out_ref[target, place : place + count, :] = latents_ref[:, first : first + 128]


def pack(w_qkv, latents):
    rows = w_qkv.shape[1]
    count, width = latents.shape
    depth = rows + rows // 2 + count * (width // 256)
    return pl.pallas_call(
        pack_kernel,
        out_shape=jax.ShapeDtypeStruct((HEADS, depth, 128), jnp.bfloat16),
        name="pack",
    )(w_qkv, latents)


def unpack_kernel(received_ref, half_ref):
    rows, width = half_ref.shape
    count = rows // HEADS
    first = received_ref.shape[1] - count * (width // 128)
    for piece in range(width // 128):
        low = first + piece * count
        half_ref[:, 128 * piece : 128 * piece + 128] = received_ref[:, low : low + count, :].reshape(
            rows, 128
        )


def unpack(received, count, width):
    return pl.pallas_call(
        unpack_kernel,
        out_shape=jax.ShapeDtypeStruct((count * HEADS, width // 2), jnp.bfloat16),
        compiler_params=limit(4),
        cost_estimate=pl.CostEstimate(
            flops=2000000000, bytes_accessed=1024, transcendentals=0
        ),
        name="unpack",
    )(received)


def point_norm_kernel(features_ref, w_embed_ref, gain_ref, out_ref):
    embedded = dot_tn(features_ref[...], w_embed_ref[...])
    out_ref[...] = norm_rows(embedded, gain_ref[...]).astype(jnp.bfloat16)


def point_norms(features, w_embed, gain):
    points, width = features.shape[1], w_embed.shape[1]
    return pl.pallas_call(
        point_norm_kernel,
        out_shape=jax.ShapeDtypeStruct((points, width), jnp.bfloat16),
        compiler_params=limit(16),
        cost_estimate=pl.CostEstimate(flops=1024, bytes_accessed=1024, transcendentals=0),
        name="point_norms",
    )(features, w_embed, gain)


def point_query_kernel(normed_ref, w_query_ref, out_ref):
    out_ref[...] = dot_nn(normed_ref[...], w_query_ref[...]).astype(jnp.bfloat16)


def point_queries(normed, w_query):
    points, width = normed.shape
    return pl.pallas_call(
        point_query_kernel,
        grid=(points // POINT_BLOCK,),
        in_specs=[
            pl.BlockSpec((POINT_BLOCK, width), lambda i: (i, 0)),
            pl.BlockSpec((width, width), lambda i: (0, 0)),
        ],
        out_specs=pl.BlockSpec((POINT_BLOCK, width), lambda i: (i, 0)),
        out_shape=jax.ShapeDtypeStruct((points, width), jnp.bfloat16),
        cost_estimate=pl.CostEstimate(flops=1024, bytes_accessed=1024, transcendentals=0),
        name="point_queries",
    )(normed, w_query)


def joined_halves(core, own, other):
    first = core == 0
    return jnp.concatenate([jnp.where(first, own, other), jnp.where(first, other, own)], axis=1)


def self_kernel(place_ref, received_ref, own_ref, other_ref, gain_ref, out_ref):
    latents = joined_halves(place_ref[1], own_ref[...], other_ref[...])
    normed = norm_rows(latents.astype(jnp.float32), gain_ref[...]).astype(jnp.bfloat16)
    width = latents.shape[1]
    rows = width // HEADS
    query_key = dot_nn(normed, received_ref[:, :rows, :].reshape(width, 2 * HEAD_DIM))
    query_key = query_key.astype(jnp.bfloat16)
    folded = received_ref[:, rows : rows + rows // 2, :]
    w_value = jnp.concatenate([folded[:, :, :HEAD_DIM], folded[:, :, HEAD_DIM:]], axis=1)
    values = dot_nn(normed, w_value.reshape(width, HEAD_DIM)).astype(jnp.bfloat16)
    scores = dot_nt(query_key[:, HEAD_DIM:], query_key[:, :HEAD_DIM]) * SCALE
    powers = jnp.exp(scores - jnp.max(scores, axis=0, keepdims=True))
    shares = (powers / jnp.sum(powers, axis=0, keepdims=True)).astype(jnp.bfloat16)
    out_ref[...] = dot_tn(values, shares).astype(jnp.bfloat16)


def self_attention(place, received, own, other, gain):
    vmem = pl.BlockSpec(memory_space=pltpu.VMEM)
    return pl.pallas_call(
        self_kernel,
        in_specs=[pl.BlockSpec(memory_space=pltpu.SMEM)] + [vmem] * 4,
        out_shape=jax.ShapeDtypeStruct((HEAD_DIM, own.shape[0]), jnp.bfloat16),
        compiler_params=limit(8),
        name="self_attention",
    )(place, received, own, other, gain)


def tail_kernel(
    place_ref, near_ref, far_ref, out_0_ref, out_1_ref, out_2_ref, out_3_ref, own_ref, other_ref,
    gain_cross_ref, w_kv_ref,
    queries_ref, features_ref, w_back_ref, w_embed_ref, gain_head_ref, w_hidden_ref, w_sdf_ref,
    decoded_ref, sdf_ref, all_decoded, key_pairs, value_rows, crossed,
):
    me, core = place_ref[0], place_ref[1]
    half_width = own_ref.shape[1]
    for side_ref, place in ((own_ref, core), (other_ref, 1 - core)):
        low = pl.multiple_of(half_width * place, half_width)
        all_decoded[:, pl.ds(low, half_width)] = side_ref[...]
    update = all_decoded[...].astype(jnp.float32)
    quarter = out_0_ref.shape[0]
    for piece, out_ref in enumerate((out_0_ref, out_1_ref, out_2_ref, out_3_ref)):
        side_ref = near_ref if piece < 2 else far_ref
        low = quarter * (piece % 2)
        heads = [
            side_ref[low + HEAD_DIM * block : low + HEAD_DIM * block + HEAD_DIM, :]
            for block in (0, 2, 1, 3)
        ]
        update += dot_tn(jnp.concatenate(heads, axis=0), out_ref[...])
    decoded = update.astype(jnp.bfloat16)
    all_decoded[...] = decoded
    rows = decoded_ref.shape[0]
    decoded_ref[...] = all_decoded[pl.ds(pl.multiple_of(me * rows, rows), rows), :]
    normed = norm_rows(decoded.astype(jnp.float32), gain_cross_ref[...]).astype(jnp.bfloat16)
    keys = dot_nn(normed, w_kv_ref[0]).astype(jnp.bfloat16) * SCALE
    key_count = keys.shape[0]
    lane = lax.broadcasted_iota(jnp.int32, (key_count, 128), 1)
    for pair in range(HEADS // 2):
        both = keys[:, 128 * pair : 128 * pair + 128]
        zero = jnp.zeros_like(both)
        key_pairs[pair, :key_count, :] = jnp.where(lane < HEAD_DIM, both, zero)
        key_pairs[pair, key_count:, :] = jnp.where(lane < HEAD_DIM, zero, both)
    values = lax.dot_general(
        w_kv_ref[1], normed, (((0,), (1,)), ((), ())), preferred_element_type=jnp.float32
    ).astype(jnp.bfloat16)
    for head in range(HEADS):
        value_rows[head, :HEAD_DIM, :] = values[HEAD_DIM * head : HEAD_DIM * head + HEAD_DIM, :]
        value_rows[head, HEAD_DIM:, :] = jnp.ones((16, key_count), jnp.bfloat16)

    for pair in range(HEADS // 2):
        scores = dot_nt(key_pairs[pair], queries_ref[:, 128 * pair : 128 * pair + 128])
        for side in range(2):
            head = 2 * pair + side
            own = scores[side * key_count : side * key_count + key_count, :]
            powers = jnp.exp(own - jnp.max(own, axis=0, keepdims=True)).astype(jnp.bfloat16)
            blended = dot_nn(value_rows[head], powers)
            crossed[HEAD_DIM * head : HEAD_DIM * head + HEAD_DIM, :] = (
                blended[:HEAD_DIM, :] / blended[HEAD_DIM : HEAD_DIM + 1, :]
            ).astype(jnp.bfloat16)

    joined = dot_tn(crossed[...], w_back_ref[...]) + dot_tn(features_ref[...], w_embed_ref[...])
    head_in = norm_rows(joined, gain_head_ref[...]).astype(jnp.bfloat16)
    hidden = jax.nn.gelu(dot_nn(head_in, w_hidden_ref[...])).astype(jnp.bfloat16)
    sdf_ref[...] = dot_nt(w_sdf_ref[...], hidden)[:1, :]


def tail(
    place, near, far, outs, own, other, gain_cross, w_kv, queries, features, w_back, w_embed,
    gain_head, w_hidden, w_sdf,
):
    points, width = queries.shape
    keys = own.shape[0]
    vmem = pl.BlockSpec(memory_space=pltpu.VMEM)
    return pl.pallas_call(
        tail_kernel,
        in_specs=[pl.BlockSpec(memory_space=pltpu.SMEM)]
        + [vmem] * 9
        + [vmem] * 8,
        out_specs=(vmem, vmem),
        out_shape=(
            jax.ShapeDtypeStruct((keys // HEADS, width), jnp.bfloat16),
            jax.ShapeDtypeStruct((1, points), jnp.float32),
        ),
        scratch_shapes=[
            pltpu.VMEM((keys, width), jnp.bfloat16),
            pltpu.VMEM((HEADS // 2, 2 * keys, 128), jnp.bfloat16),
            pltpu.VMEM((HEADS, HEAD_DIM + 16, keys), jnp.bfloat16),
            pltpu.VMEM((width, points), jnp.bfloat16),
        ],
        compiler_params=limit(TAIL_LIMIT),
        name="tail",
    )(
        place, near, far, *outs, own, other, gain_cross, w_kv, queries, features, w_back, w_embed,
        gain_head, w_hidden, w_sdf,
    )


def swap(values, bit, count):
    return lax.ppermute(values, "query", [(i, i ^ bit) for i in range(count)])


def to_all(blocks):
    return lax.all_to_all(blocks, "query", split_axis=0, concat_axis=0, tiled=True)


def after(values, *others):
    return lax.optimization_barrier((values, *others))[0]


def one_head_each(
    latents, gain_self, w_qkv, w_out, gain_cross, w_kv, w_embed, gain_point, w_query, w_back,
    gain_head, w_hidden, w_sdf, *, points, count,
):
    me = lax.axis_index("query")
    place = jnp.stack([me, me & 1])
    received = to_all(pack(w_qkv, latents))

    numbers = me * points + jnp.arange(points, dtype=jnp.int32)
    features = feature_rows(numbers)
    features = jnp.pad(features, ((0, FEATURE_ROWS - features.shape[0]), (0, 0)))
    w_embed = jnp.pad(w_embed, ((0, FEATURE_ROWS - w_embed.shape[0]), (0, 0)))
    sdf_row = jnp.pad(w_sdf[None, :], ((0, 15), (0, 0)))
    out = jnp.concatenate([w_out, swap(w_out, EXCHANGES[0], count)], axis=0)
    out_swapped = swap(out, EXCHANGES[1], count)
    normed = point_norms(after(features, out), w_embed, gain_point[None, :])
    queries = point_queries(normed, w_query)
    out_0 = jnp.concatenate([out, after(out_swapped, queries)], axis=0)
    out_1 = swap(out_0, EXCHANGES[2], count)

    received, queries, features, w_embed, sdf_row, place, out_0 = lax.optimization_barrier(
        (received, queries, features, w_embed, sdf_row, place, out_0)
    )
    own = unpack(received, latents.shape[0], latents.shape[1])
    other = swap(own, 1, count)
    out_2 = swap(after(out_0, own), EXCHANGES[3], count)
    attended = self_attention(place, received, own, other, gain_self[None, :])
    near = attended
    for bit in HEAD_EXCHANGES[:3]:
        near = jnp.concatenate([near, swap(near, bit, count)], axis=0)
    out_3 = swap(out_1, EXCHANGES[3], count)
    far = swap(near, HEAD_EXCHANGES[3], count)
    decoded, sdf = tail(
        place, near, far, (out_0, out_1, out_2, out_3), own, other, gain_cross[None, :], w_kv,
        queries, features, w_back, w_embed, gain_head[None, :], w_hidden, sdf_row,
    )
    return decoded, sdf[0]


def solution(mesh):
    parts, count = mesh.shape["shape"], mesh.shape["query"]

    def program(latents, *others):
        own = latents.shape[0] // (parts * count)
        points = 1024
        shards = functools.partial(any_slice, points=points)
        if count == HEADS and own == 16 and others[1].shape[1] // count == 64:
            shards = functools.partial(one_head_each, points=points, count=count)
        return jax.shard_map(
            shards,
            mesh=mesh,
            in_specs=(
                P(("shape", "query"), None),
                P(),
                P(None, "query", None),
                P("query", None),
                P(),
                P(),
                P(),
                P(),
                P(),
                P(),
                P(),
                P(),
                P(),
            ),
            out_specs=(P(("shape", "query"), None), P(("shape", "query"))),
            check_vma=False,
        )(latents, *others)

    return program
```
